512 devices in a mesh: tm: 8 (over y), rows: 64 (over z, x, core).
Axes of the slice: x: 4, y: 8, z: 8, core: 2. Of those that a mesh axis runs over, the one named last changes fastest.
Arguments:
- latent: bfloat16 [16, 64, 32, 384], P('tm', 'rows'), may hold values from -6 to 6
- gain_one: float32 [384], replicated, may hold values from 0.1 to 1.9
- weight_one: bfloat16 [3, 3, 3, 384, 384], P(None, None, None, None, 'rows'), may hold values from -0.0625 to 0.0625
- bias_one: float32 [384], replicated, may hold values from -1.2 to 1.2
- gain_two: float32 [384], replicated, may hold values from 0.1 to 1.9
- weight_two: bfloat16 [3, 3, 3, 384, 384], P(None, None, None, None, 'rows'), may hold values from -0.0625 to 0.0625
- bias_two: float32 [384], replicated, may hold values from -1.2 to 1.2
Outputs:
- block_out: bfloat16 [16, 64, 32, 384], P('tm', 'rows')
The draws below stay inside these ranges and needn't reach their ends.
All inputs are finite; a program needn't handle non-finite values.
Results may differ from the reference program's by a relative error of at most 0.01.
Values may be sent and summed in bfloat16 or wider, within the bound.
No kernel may reach another device: no remote copies, remote signals or barrier semaphores. Data moves between devices by JAX's collectives and lax.ppermute only.
A program may use at most 128 MiB of HBM per device.

```python
import jax
import jax.numpy as jnp
from jax import lax

C = 384
W = 32
FRAMES = 16
HEIGHT = 64


def steps_of(own_key, shape, pieces, least, largest):
    factor_of = 1.0
    for position, parts in pieces:
        steps = jax.random.uniform(jax.random.fold_in(jax.random.fold_in(own_key, 6), position), (parts,), jnp.float32, least / len(pieces), largest / len(pieces))
        factor_of = factor_of * jnp.repeat(jnp.exp(steps), shape[position] // parts).reshape((-1,) + (1,) * (len(shape) - 1 - position))
    return factor_of


def centred(stream_key, shape, deviation, limit, cuts=(), held_as=jnp.bfloat16):
    level = steps_of(stream_key, shape, cuts, -0.22, 0.18) if cuts else 1.0
    drawn = jax.random.normal(stream_key, shape, jnp.float32) * deviation * level
    return jnp.minimum(jnp.maximum(drawn, -limit), limit).astype(held_as)


def setup_inputs(seed: int = 0) -> dict:
    streams_of = jax.random.split(jax.random.key(seed), 8)
    return {
        "latent": centred(streams_of[0], (FRAMES, HEIGHT, W, C), 1.0, 6.0, ((0, 8), (1, 64))),
        "gain_one": jnp.clip(1.0 + 0.18 * jax.random.normal(streams_of[1], (C,), jnp.float32), 0.1, 1.9),
        "weight_one": centred(streams_of[2], (3, 3, 3, C, C), (27 * C) ** -0.5, 0.0625, ((4, 64),)),
        "bias_one": centred(streams_of[3], (C,), 0.3, 1.2, (), jnp.float32),
        "gain_two": jnp.clip(1.0 + 0.18 * jax.random.normal(streams_of[4], (C,), jnp.float32), 0.1, 1.9),
        "weight_two": centred(streams_of[5], (3, 3, 3, C, C), (27 * C) ** -0.5, 0.0625, ((4, 64),)),
        "bias_two": centred(streams_of[6], (C,), 0.3, 1.2, (), jnp.float32),
    }


def rms_silu(values, gain):
    square_mean = lax.optimization_barrier(jnp.mean(values * values, axis=-1, keepdims=True))
    normed = values * lax.rsqrt(square_mean + 1e-06) * gain
    return jax.nn.silu(normed).astype(jnp.bfloat16)

def causal_conv(field, weight):
    frames, height, width, channels = field.shape
    padded = jnp.pad(field, ((2, 0), (1, 1), (1, 1), (0, 0)))
    total = jnp.zeros((frames * height * width, weight.shape[4]), jnp.float32)
    for tap_t in range(3):
        for tap_h in range(3):
            for tap_w in range(3):
                window = padded[tap_t:tap_t + frames, tap_h:tap_h + height, tap_w:tap_w + width]
                total = total + jnp.dot(window.reshape(-1, channels), weight[tap_t, tap_h, tap_w], preferred_element_type=jnp.float32)
    return total.reshape(frames, height, width, -1)

def reference(latent, gain_one, weight_one, bias_one, gain_two, weight_two, bias_two):
    hidden_one = rms_silu(latent.astype(jnp.float32), gain_one)
    middle = (causal_conv(hidden_one, weight_one) + bias_one).astype(jnp.bfloat16)
    hidden_two = rms_silu(middle.astype(jnp.float32), gain_two)
    result = latent.astype(jnp.float32) + causal_conv(hidden_two, weight_two) + bias_two
    return result.astype(jnp.bfloat16)
```

```python
import jax
import jax.numpy as jnp
from jax import lax
from jax.experimental import pallas as pl
from jax.experimental.pallas import tpu as pltpu
from jax.sharding import Mesh
from jax.sharding import PartitionSpec as P

CHANNELS = 384
BLOCK = 48
SLOT = 224
LANES = 512
VMEM = 48 * 1024 * 1024
F32 = jnp.float32
BF16 = jnp.bfloat16


def call(kernel, out_shape, scratch=(), smem=0, n=0):
    specs = [pl.BlockSpec(memory_space=pltpu.SMEM)] * smem
    specs += [pl.BlockSpec(memory_space=pltpu.VMEM)] * (n - smem)
    multiple = isinstance(out_shape, (list, tuple))
    vmem = pl.BlockSpec(memory_space=pltpu.VMEM)
    return pl.pallas_call(
        kernel,
        out_shape=out_shape,
        in_specs=specs,
        out_specs=[vmem] * len(out_shape) if multiple else vmem,
        scratch_shapes=list(scratch),
        compiler_params=pltpu.CompilerParams(vmem_limit_bytes=VMEM),
    )


def shape(dims, dtype):
    return jax.ShapeDtypeStruct(dims, dtype)


def silu(v):
    return v / (1.0 + jnp.exp(-v))


def prepare_kernel(latent, gain, weight_one, weight_two, hidden, slot_one, slot_two, rows):
    values = latent[...].astype(F32)
    mean = jnp.mean(values * values, axis=1, keepdims=True)
    result = silu(values * lax.rsqrt(mean + 1e-6) * gain[...]).astype(BF16)
    for z in range(8):
        hidden[z] = result
    for weight, slot in ((weight_one, slot_one), (weight_two, slot_two)):
        rows[...] = jnp.zeros_like(rows)
        for tap in range(27):
            rows[8 * tap : 8 * tap + 6, :] = weight[tap].astype(F32)
        slot[...] = rows[...].astype(BF16)


def place_weights(ids, own, ahead, behind, across, swapped, whole):
    x, c = ids[1], ids[2]
    for shift, piece in ((0, own), (1, ahead), (2, across), (3, behind)):
        position = lax.rem(x + 4 - shift, 4) * 2
        whole[position + c] = piece[...]
        whole[position + 1 - c] = swapped[shift]


def taps(ids, products, keep, partner, pair):
    c = ids[2]
    column = lax.rem(lax.broadcasted_iota(jnp.int32, (8, 2 * LANES), 1), 32)
    half = LANES // 2
    for two in range(4):
        parts = ([], [], [])
        for slot in (2 * two, 2 * two + 1):
            for j in range(3):
                sums = []
                for l in range(3):
                    k = [
                        products[pl.ds(slot * SLOT + 8 * (9 * i + 3 * j + l), 8), :]
                        for i in range(3)
                    ]
                    sums.append(
                        jnp.concatenate(
                            [
                                k[2][:, :half],
                                k[2][:, half:] + k[1][:, :half],
                                k[1][:, half:] + k[0][:, :half],
                                k[0][:, half:],
                            ],
                            axis=1,
                        )
                    )
                left = jnp.where(column == 0, 0.0, pltpu.roll(sums[0], 1, 1))
                right = jnp.where(column == 31, 0.0, pltpu.roll(sums[2], 2 * LANES - 1, 1))
                parts[j].append(sums[1] + left + right)
        below, level, above = [jnp.concatenate(p, axis=0) for p in parts]
        at = pl.ds(16 * two, 16)
        keep[at, :] = level
        partner[at, :] = jnp.where(c == 0, below, above).astype(BF16)
        pair[at, :] = jnp.where(c == 0, above, below).astype(BF16)


def conv_one_kernel(ids, gathered, own, ahead, behind, across, swapped, keep, partner, pair, whole, field, products):
    place_weights(ids, own, ahead, behind, across, swapped, whole)
    for z in range(8):
        for f in range(2):
            field[pl.ds(256 * f + 32 * z, 32), :] = gathered[z, pl.ds(32 * f, 32), :]
    products[...] = lax.dot_general(
        whole[...].reshape(8 * SLOT, CHANNELS),
        field[...],
        (((1,), (1,)), ((), ())),
        preferred_element_type=F32,
    )
    taps(ids, products, keep, partner, pair)


def conv_two_kernel(ids, gathered, gain, own, ahead, behind, across, swapped, keep, partner, pair, whole, products):
    place_weights(ids, own, ahead, behind, across, swapped, whole)
    values = gathered[...].reshape(CHANNELS, LANES).astype(F32)
    mean = jnp.mean(values * values, axis=0, keepdims=True)
    square = (CHANNELS, CHANNELS)
    same = lax.broadcasted_iota(jnp.int32, square, 0) == lax.broadcasted_iota(jnp.int32, square, 1)
    scale = jnp.sum(jnp.where(same, gain[...], 0.0), axis=1, keepdims=True)
    hidden = silu(values * lax.rsqrt(mean + 1e-6) * scale).astype(BF16)
    products[...] = jnp.dot(
        whole[...].reshape(8 * SLOT, CHANNELS), hidden, preferred_element_type=F32
    )
    taps(ids, products, keep, partner, pair)


def rows_kernel(ids, keep, partner, pair, own, later):
    position = 2 * ids[1] + ids[2]
    got = pair[...].astype(F32)
    place = lax.rem(lax.broadcasted_iota(jnp.int32, got.shape, 1) // 32, 8)
    down = jnp.where(place == 0, 0.0, pltpu.roll(got, 32, 1))
    up = jnp.where(place == 7, 0.0, pltpu.roll(got, 2 * LANES - 32, 1))
    got = jnp.where(position == 0, down, jnp.where(position == 7, up, got))
    total = keep[...] + partner[...].astype(F32) + got
    own[...] = total[:, :LANES]
    later[...] = total[:, LANES:].astype(BF16)


def block_values(ids, own, earlier, bias):
    row = lax.broadcasted_iota(jnp.int32, (64, CHANNELS), 0)
    channel = lax.broadcasted_iota(jnp.int32, (64, CHANNELS), 1)
    wanted = BLOCK * ids[0] + 6 * (row // 8) + lax.rem(row, 8)
    chosen = (channel == wanted) & (lax.rem(row, 8) < 6)
    column = jnp.sum(jnp.where(chosen, bias[...], 0.0), axis=1, keepdims=True)
    total = (own[...] + earlier[...].astype(F32) + column).astype(BF16)
    to = lax.broadcasted_iota(jnp.int32, (BLOCK, 64), 0)
    frm = lax.broadcasted_iota(jnp.int32, (BLOCK, 64), 1)
    pick = (frm == 8 * (to // 6) + lax.rem(to, 6)).astype(BF16)
    return jnp.dot(pick, total, preferred_element_type=F32).astype(BF16)


def middle_kernel(ids, own, earlier, bias, middle):
    result = block_values(ids, own, earlier, bias)
    for z in range(8):
        middle[z] = result


def spread_kernel(ids, own, earlier, bias, pieces):
    result = block_values(ids, own, earlier, bias)
    for z in range(8):
        frames = [result[:, 256 * f + 32 * z : 256 * f + 32 * z + 32] for f in range(2)]
        pieces[z] = jnp.concatenate(frames, axis=1)


def finish_kernel(latent, gathered, out):
    square = (CHANNELS, CHANNELS)
    same = lax.broadcasted_iota(jnp.int32, square, 0) == lax.broadcasted_iota(jnp.int32, square, 1)
    conv = lax.dot_general(
        gathered[...].reshape(CHANNELS, 64),
        same.astype(BF16),
        (((0,), (0,)), ((), ())),
        preferred_element_type=F32,
    )
    out[...] = (latent[...].astype(F32) + conv).astype(BF16)


def gather_weights(slot):
    shifted = [
        lax.ppermute(slot, "x", [(i, (i + by) % 4) for i in range(4)]) for by in (1, 2, 3)
    ]
    own = jnp.stack([slot] + shifted)
    swapped = lax.ppermute(own, "core", [(0, 1), (1, 0)])
    return slot, shifted[0], shifted[2], shifted[1], swapped


def exchange(ids, keep, partner, pair):
    partner = lax.ppermute(partner, "core", [(0, 1), (1, 0)])
    swaps = []
    for x in range(4):
        swaps += [(2 * x + 1, 2 * ((x + 1) % 4)), (2 * ((x + 1) % 4), 2 * x + 1)]
    pair = lax.ppermute(pair, ("x", "core"), swaps)
    own, later = call(
        rows_kernel,
        [shape((64, LANES), F32), shape((64, LANES), BF16)],
        smem=1,
        n=4,
    )(ids, keep, partner, pair)
    earlier = lax.ppermute(later, "t", [(i, i + 1) for i in range(7)])
    return own, earlier


def per_device(latent, gain_one, weight_one, bias_one, gain_two, weight_two, bias_two):
    ids = jnp.stack([lax.axis_index(a) for a in ("z", "x", "core")]).astype(jnp.int32)
    latent = latent.reshape(64, CHANNELS)
    weight_one, weight_two = [
        jnp.transpose(w, (0, 1, 2, 4, 3)).reshape(27, 6, CHANNELS)
        for w in (weight_one, weight_two)
    ]
    gain_one, bias_one, gain_two, bias_two = [
        v.reshape(1, CHANNELS) for v in (gain_one, bias_one, gain_two, bias_two)
    ]
    slot = shape((SLOT, CHANNELS), BF16)
    hidden, slot_one, slot_two = call(
        prepare_kernel,
        [shape((8, 64, CHANNELS), BF16), slot, slot],
        [pltpu.VMEM((SLOT, CHANNELS), F32)],
        n=4,
    )(latent, gain_one, weight_one, weight_two)
    weights_one = gather_weights(slot_one)
    hidden = lax.all_to_all(hidden, "z", 0, 0)
    weights_two = gather_weights(slot_two)

    sums = [
        shape((64, 2 * LANES), F32),
        shape((64, 2 * LANES), BF16),
        shape((64, 2 * LANES), BF16),
    ]
    whole = pltpu.VMEM((8, SLOT, CHANNELS), BF16)
    products = pltpu.VMEM((8 * SLOT, LANES), F32)
    sums_one = call(
        conv_one_kernel,
        sums,
        [whole, pltpu.VMEM((LANES, CHANNELS), BF16), products],
        smem=1,
        n=7,
    )(ids, hidden, *weights_one)
    own, earlier = exchange(ids, *sums_one)
    middle = call(middle_kernel, shape((8, BLOCK, LANES), BF16), smem=1, n=4)(
        ids, own, earlier, bias_one
    )
    middle = lax.all_to_all(middle, "z", 0, 0)
    sums_two = call(conv_two_kernel, sums, [whole, products], smem=1, n=8)(
        ids, middle, gain_two, *weights_two
    )
    own, earlier = exchange(ids, *sums_two)
    pieces = call(spread_kernel, shape((8, BLOCK, 64), BF16), smem=1, n=4)(
        ids, own, earlier, bias_two
    )
    pieces = lax.all_to_all(pieces, "z", 0, 0)
    out = call(finish_kernel, shape((64, CHANNELS), BF16), n=2)(latent, pieces)
    return out.reshape(2, 1, 32, CHANNELS)


def solution(mesh):
    mesh = Mesh(mesh.devices.reshape(8, 8, 4, 2), ("t", "z", "x", "core"))
    rows = ("z", "x", "core")
    kernel = P(None, None, None, None, rows)
    field = P("t", rows, None, None)
    return jax.shard_map(
        per_device,
        mesh=mesh,
        in_specs=(field, P(), kernel, P(), P(), kernel, P()),
        out_specs=field,
        check_vma=False,
    )
```

```python
import functools

import jax
import jax.numpy as jnp
from jax import lax
from jax.experimental import pallas as pl
from jax.experimental.pallas import tpu as pltpu
from jax.sharding import Mesh
from jax.sharding import PartitionSpec as P

CHANNELS = 384
BLOCK = 48
PIECE = 176
SLOT = 80
DEPTH = 3 * CHANNELS
LANES = 512
VMEM = 48 * 1024 * 1024
LONG = 10**11
F32 = jnp.float32
BF16 = jnp.bfloat16


def call(kernel, out_shape, scratch=(), smem=0, anywhere=0, n=0, flops=0):
    specs = [pl.BlockSpec(memory_space=pltpu.SMEM)] * smem
    specs += [pl.BlockSpec(memory_space=pl.ANY)] * anywhere
    specs += [pl.BlockSpec(memory_space=pltpu.VMEM)] * (n - len(specs))
    multiple = isinstance(out_shape, (list, tuple))
    vmem = pl.BlockSpec(memory_space=pltpu.VMEM)
    return pl.pallas_call(
        kernel,
        out_shape=out_shape,
        in_specs=specs,
        out_specs=[vmem] * len(out_shape) if multiple else vmem,
        scratch_shapes=list(scratch),
        compiler_params=pltpu.CompilerParams(vmem_limit_bytes=VMEM),
        cost_estimate=pl.CostEstimate(flops=flops, bytes_accessed=0, transcendentals=0),
    )


def shape(dims, dtype):
    return jax.ShapeDtypeStruct(dims, dtype)


def iota(dims, axis):
    return lax.broadcasted_iota(jnp.int32, dims, axis)


def silu(v):
    return v / (1.0 + jnp.exp(-v))


def norm_kernel(latent, gain, hidden):
    values = latent[...].astype(F32)
    mean = jnp.mean(values * values, axis=1, keepdims=True)
    scale = lax.rsqrt(mean + 1e-6) * gain[...].reshape(1, CHANNELS)
    result = silu(values * scale).astype(BF16)
    for z in range(8):
        hidden[z] = result


def prepare_kernel(after, weight, piece, rows):
    for tap in range(27):
        rows[6 * tap : 6 * tap + 6, :] = weight[tap].astype(F32)
    rows[162:PIECE, :] = jnp.zeros((PIECE - 162, CHANNELS), F32)
    piece[...] = rows[...].astype(BF16)


def place_weights(ids, own, ahead, behind, across, swapped, whole):
    x, c = ids[1], ids[2]
    row = iota((3 * SLOT, PIECE), 0)
    j, a, k = row // SLOT, lax.rem(row, SLOT) // 8, lax.rem(row, 8)
    source = 6 * (9 * (a // 3) + 3 * j + lax.rem(a, 3)) + k
    wanted = (source == iota((3 * SLOT, PIECE), 1)) & (a < 9) & (k < 6)
    spread = wanted.astype(F32).astype(BF16)

    def place(position, value):
        rows = jnp.dot(spread, value, preferred_element_type=F32).astype(BF16)
        at = pl.ds(pl.multiple_of(position * SLOT, 16), SLOT)
        for j in range(3):
            whole[at, pl.ds(CHANNELS * j, CHANNELS)] = rows[SLOT * j : SLOT * j + SLOT]

    for shift, piece in ((0, own), (1, ahead), (2, across), (3, behind)):
        position = lax.rem(x + 4 - shift, 4) * 2
        place(position + c, piece[...])
        place(position + 1 - c, swapped[shift])


def taps(products, own, later):
    column = lax.rem(iota((8, 2 * LANES), 1), 32)
    half = LANES // 2
    for two in range(4):
        rows = []
        for slot in (2 * two, 2 * two + 1):
            sums = []
            for l in range(3):
                k = [products[pl.ds(slot * SLOT + 8 * (3 * i + l), 8), :] for i in range(3)]
                parts = [
                    k[2][:, :half],
                    k[2][:, half:] + k[1][:, :half],
                    k[1][:, half:] + k[0][:, :half],
                    k[0][:, half:],
                ]
                sums.append(jnp.concatenate(parts, axis=1))
            left = jnp.where(column == 0, 0.0, pltpu.roll(sums[0], 1, 1))
            right = jnp.where(column == 31, 0.0, pltpu.roll(sums[2], 2 * LANES - 1, 1))
            rows.append(sums[1] + left + right)
        both = jnp.concatenate(rows, axis=0)
        at = pl.ds(16 * two, 16)
        own[at, :] = both[:, :LANES]
        later[at, :] = both[:, LANES:].astype(BF16)


def conv_one_kernel(ids, level, partner, pair, *rest):
    *pieces, own, later, whole, field, products = rest
    place_weights(ids, *pieces, whole)
    c = ids[2]
    position = 2 * ids[1] + c
    step = jnp.where(position == 0, -1, jnp.where(position == 7, 1, 0))
    for z in range(8):
        other = z + step
        inside = ((other >= 0) & (other < 8)).astype(BF16)
        beyond = pair[jnp.clip(other, 0, 7)] * inside

        def put(j, value):
            for f in range(2):
                at = pl.ds(256 * f + 32 * z, 32)
                field[at, pl.ds(CHANNELS * j, CHANNELS)] = value[32 * f : 32 * f + 32]

        put(1, level[z])

        @pl.when(c == 0)
        def _():
            put(0, beyond)
            put(2, partner[z])

        @pl.when(c == 1)
        def _():
            put(0, partner[z])
            put(2, beyond)

    products[...] = lax.dot_general(
        whole[...], field[...], (((1,), (1,)), ((), ())), preferred_element_type=F32
    )
    taps(products, own, later)


def field_two_kernel(gathered, gain, field):
    values = gathered[...].reshape(CHANNELS, LANES).astype(F32)
    mean = jnp.mean(values * values, axis=0, keepdims=True)
    square = (CHANNELS, CHANNELS)
    same = iota(square, 0) == iota(square, 1)
    gains = jnp.where(same, gain[...].reshape(1, CHANNELS), 0.0)
    scale = jnp.sum(gains, axis=1, keepdims=True)
    field[...] = silu(values * lax.rsqrt(mean + 1e-6) * scale).astype(BF16)


def conv_two_kernel(ids, level, partner, pair, *rest):
    *pieces, own, later, whole, field, products = rest
    place_weights(ids, *pieces, whole)
    c = ids[2]
    position = 2 * ids[1] + c
    field[pl.ds(CHANNELS, CHANNELS), :] = level[...]
    at_pair = pl.ds(pl.multiple_of(2 * CHANNELS * c, CHANNELS), CHANNELS)
    at_partner = pl.ds(pl.multiple_of(2 * CHANNELS * (1 - c), CHANNELS), CHANNELS)
    field[at_partner, :] = partner[...]
    place = lax.rem(iota((CHANNELS, LANES), 1) // 32, 8)

    @pl.when((position > 0) & (position < 7))
    def _():
        field[at_pair, :] = pair[...]

    @pl.when(position == 0)
    def _():
        moved = pltpu.roll(pair[...].astype(F32), 32, 1)
        field[at_pair, :] = jnp.where(place == 0, 0.0, moved).astype(BF16)

    @pl.when(position == 7)
    def _():
        moved = pltpu.roll(pair[...].astype(F32), LANES - 32, 1)
        field[at_pair, :] = jnp.where(place == 7, 0.0, moved).astype(BF16)

    products[...] = jnp.dot(whole[...], field[...], preferred_element_type=F32)
    taps(products, own, later)


def block_values(ids, own, earlier, bias):
    row = iota((64, CHANNELS), 0)
    wanted = BLOCK * ids[0] + 6 * (row // 8) + lax.rem(row, 8)
    chosen = (iota((64, CHANNELS), 1) == wanted) & (lax.rem(row, 8) < 6)
    biases = jnp.where(chosen, bias[...].reshape(1, CHANNELS), 0.0)
    column = jnp.sum(biases, axis=1, keepdims=True)
    total = (own[...] + earlier[...].astype(F32) + column).astype(BF16)
    to, frm = iota((BLOCK, 64), 0), iota((BLOCK, 64), 1)
    pick = (frm == 8 * (to // 6) + lax.rem(to, 6)).astype(BF16)
    return jnp.dot(pick, total, preferred_element_type=F32).astype(BF16)


def middle_kernel(ids, own, earlier, bias, middle):
    result = block_values(ids, own, earlier, bias)
    for z in range(8):
        middle[z] = result


def spread_kernel(ids, own, earlier, bias, latent, pieces, kept):
    result = block_values(ids, own, earlier, bias)
    for z in range(8):
        frames = [result[:, 256 * f + 32 * z : 256 * f + 32 * z + 32] for f in range(2)]
        pieces[z] = jnp.concatenate(frames, axis=1)
    kept[...] = latent[...]


def finish_kernel(latent, gathered, out):
    square = (CHANNELS, CHANNELS)
    same = iota(square, 0) == iota(square, 1)
    conv = lax.dot_general(
        gathered[...].reshape(CHANNELS, 64),
        same.astype(BF16),
        (((0,), (0,)), ((), ())),
        preferred_element_type=F32,
    )
    out[...] = (latent[...].astype(F32) + conv).astype(BF16)


def swap_cores(value):
    return lax.ppermute(value, "core", [(0, 1), (1, 0)])


def swap_chips(value):
    pairs = []
    for x in range(4):
        last, first = 2 * x + 1, 2 * ((x + 1) % 4)
        pairs += [(last, first), (first, last)]
    return lax.ppermute(value, ("x", "core"), pairs)


def pack_kernel(own, one, two, three, out):
    for i, piece in enumerate((own, one, two, three)):
        out[i] = piece[...]


def gather_weights(piece):
    one, two, three = [
        lax.ppermute(piece, "x", [(i, (i + by) % 4) for i in range(4)]) for by in (1, 2, 3)
    ]
    packed = call(pack_kernel, shape((4, PIECE, CHANNELS), BF16), n=4)(piece, one, two, three)
    return piece, one, three, two, swap_cores(packed)


def per_device(latent, gain_one, weight_one, bias_one, gain_two, weight_two, bias_two):
    ids = jnp.stack([lax.axis_index(a) for a in ("z", "x", "core")]).astype(jnp.int32)
    latent = latent.reshape(64, CHANNELS)
    weight_one, weight_two = [
        jnp.transpose(w, (0, 1, 2, 4, 3)).reshape(27, 6, CHANNELS)
        for w in (weight_one, weight_two)
    ]
    prepare = call(
        prepare_kernel,
        shape((PIECE, CHANNELS), BF16),
        [pltpu.VMEM((PIECE, CHANNELS), F32)],
        anywhere=1,
        n=2,
    )
    sums = [shape((64, LANES), F32), shape((64, LANES), BF16)]
    whole = pltpu.VMEM((8 * SLOT, DEPTH), BF16)
    products = pltpu.VMEM((8 * SLOT, LANES), F32)
    later_to_next = lambda v: lax.ppermute(v, "t", [(i, i + 1) for i in range(7)])

    hidden = call(norm_kernel, shape((8, 64, CHANNELS), BF16), n=2)(latent, gain_one)
    weights = gather_weights(prepare(hidden, weight_one))
    level = lax.all_to_all(hidden, "z", 0, 0)
    own, later = call(
        conv_one_kernel,
        sums,
        [whole, pltpu.VMEM((LANES, DEPTH), BF16), products],
        smem=1,
        n=9,
    )(ids, level, swap_cores(level), swap_chips(level), *weights)
    middle = call(middle_kernel, shape((8, BLOCK, LANES), BF16), smem=1, n=4)(
        ids, own, later_to_next(later), bias_one
    )

    weights = gather_weights(prepare(middle, weight_two))
    level = call(field_two_kernel, shape((CHANNELS, LANES), BF16), n=2)(
        lax.all_to_all(middle, "z", 0, 0), gain_two
    )
    own, later = call(
        conv_two_kernel,
        sums,
        [whole, pltpu.VMEM((DEPTH, LANES), BF16), products],
        smem=1,
        n=9,
    )(ids, level, swap_cores(level), swap_chips(level), *weights)
    pieces, kept = call(
        spread_kernel,
        [shape((8, BLOCK, 64), BF16), shape((64, CHANNELS), BF16)],
        smem=1,
        n=5,
    )(ids, own, later_to_next(later), bias_two, latent)
    pieces = lax.all_to_all(pieces, "z", 0, 0)
    out = call(finish_kernel, shape((64, CHANNELS), BF16), n=2)(kept, pieces)
    return out.reshape(2, 1, 32, CHANNELS)


def solution(mesh):
    mesh = Mesh(mesh.devices.reshape(8, 8, 4, 2), ("t", "z", "x", "core"))
    rows = ("z", "x", "core")
    kernel = P(None, None, None, None, rows)
    field = P("t", rows, None, None)
    return jax.shard_map(
        per_device,
        mesh=mesh,
        in_specs=(field, P(), kernel, P(), P(), kernel, P()),
        out_specs=field,
        check_vma=False,
    )
```

```python
import jax
import jax.numpy as jnp
from jax import lax
from jax.experimental import pallas as pl
from jax.experimental.pallas import tpu as pltpu
from jax.sharding import Mesh
from jax.sharding import PartitionSpec as P

CHANNELS = 384
BLOCK = 48
PIECE = 176
SLOT = 224
LANES = 512
VMEM = 48 * 1024 * 1024
F32 = jnp.float32
BF16 = jnp.bfloat16


def call(kernel, out_shape, scratch=(), smem=0, anywhere=0, n=0, flops=0):
    specs = [pl.BlockSpec(memory_space=pltpu.SMEM)] * smem
    specs += [pl.BlockSpec(memory_space=pl.ANY)] * anywhere
    specs += [pl.BlockSpec(memory_space=pltpu.VMEM)] * (n - len(specs))
    multiple = isinstance(out_shape, (list, tuple))
    vmem = pl.BlockSpec(memory_space=pltpu.VMEM)
    return pl.pallas_call(
        kernel,
        out_shape=out_shape,
        in_specs=specs,
        out_specs=[vmem] * len(out_shape) if multiple else vmem,
        scratch_shapes=list(scratch),
        compiler_params=pltpu.CompilerParams(vmem_limit_bytes=VMEM),
        cost_estimate=pl.CostEstimate(flops=flops, bytes_accessed=0, transcendentals=0),
    )


def shape(dims, dtype):
    return jax.ShapeDtypeStruct(dims, dtype)


def iota(dims, axis):
    return lax.broadcasted_iota(jnp.int32, dims, axis)


def silu(v):
    return v / (1.0 + jnp.exp(-v))


def norm_kernel(latent, gain, hidden):
    values = latent[...].astype(F32)
    mean = jnp.mean(values * values, axis=1, keepdims=True)
    scale = lax.rsqrt(mean + 1e-6) * gain[...].reshape(1, CHANNELS)
    result = silu(values * scale).astype(BF16)
    for z in range(8):
        hidden[z] = result


def prepare_kernel(weight_one, weight_two, piece_one, piece_two, rows):
    for weight, piece in ((weight_one, piece_one), (weight_two, piece_two)):
        for tap in range(27):
            rows[6 * tap : 6 * tap + 6, :] = weight[tap].astype(F32)
        rows[162:PIECE, :] = jnp.zeros((PIECE - 162, CHANNELS), F32)
        piece[...] = rows[...].astype(BF16)


def place_weights(ids, own, ahead, behind, across, swapped, whole):
    x, c = ids[1], ids[2]
    row = iota((SLOT, PIECE), 0)
    wanted = (iota((SLOT, PIECE), 1) == 6 * (row // 8) + lax.rem(row, 8)) & (lax.rem(row, 8) < 6)
    spread = wanted.astype(F32).astype(BF16)

    def place(position, value):
        whole[position] = jnp.dot(spread, value, preferred_element_type=F32).astype(BF16)

    for shift, piece in ((0, own), (1, ahead), (2, across), (3, behind)):
        position = lax.rem(x + 4 - shift, 4) * 2
        place(position + c, piece[...])
        place(position + 1 - c, swapped[shift])


def taps(ids, products, keep, partner, pair):
    c = ids[2]
    column = lax.rem(iota((8, 2 * LANES), 1), 32)
    half = LANES // 2
    for two in range(4):
        parts = ([], [], [])
        for slot in (2 * two, 2 * two + 1):
            for j in range(3):
                sums = []
                for l in range(3):
                    k = [
                        products[pl.ds(slot * SLOT + 8 * (9 * i + 3 * j + l), 8), :]
                        for i in range(3)
                    ]
                    frames = [
                        k[2][:, :half],
                        k[2][:, half:] + k[1][:, :half],
                        k[1][:, half:] + k[0][:, :half],
                        k[0][:, half:],
                    ]
                    sums.append(jnp.concatenate(frames, axis=1))
                left = jnp.where(column == 0, 0.0, pltpu.roll(sums[0], 1, 1))
                right = jnp.where(column == 31, 0.0, pltpu.roll(sums[2], 2 * LANES - 1, 1))
                parts[j].append(sums[1] + left + right)
        below, level, above = [jnp.concatenate(p, axis=0) for p in parts]
        at = pl.ds(16 * two, 16)
        keep[at, :] = level
        partner[at, :] = jnp.where(c == 0, below, above).astype(BF16)
        pair[at, :] = jnp.where(c == 0, above, below).astype(BF16)


def conv_one_kernel(ids, gathered, *rest):
    *pieces, keep, partner, pair, whole, field, products = rest
    place_weights(ids, *pieces, whole)
    for z in range(8):
        for f in range(2):
            field[pl.ds(256 * f + 32 * z, 32), :] = gathered[z, pl.ds(32 * f, 32), :]
    products[...] = lax.dot_general(
        whole[...].reshape(8 * SLOT, CHANNELS),
        field[...],
        (((1,), (1,)), ((), ())),
        preferred_element_type=F32,
    )
    taps(ids, products, keep, partner, pair)


def conv_two_kernel(ids, gathered, gain, *rest):
    *pieces, keep, partner, pair, whole, products = rest
    place_weights(ids, *pieces, whole)
    values = gathered[...].reshape(CHANNELS, LANES).astype(F32)
    mean = jnp.mean(values * values, axis=0, keepdims=True)
    square = (CHANNELS, CHANNELS)
    same = iota(square, 0) == iota(square, 1)
    gains = jnp.where(same, gain[...].reshape(1, CHANNELS), 0.0)
    scale = jnp.sum(gains, axis=1, keepdims=True)
    field = silu(values * lax.rsqrt(mean + 1e-6) * scale).astype(BF16)
    products[...] = jnp.dot(
        whole[...].reshape(8 * SLOT, CHANNELS), field, preferred_element_type=F32
    )
    taps(ids, products, keep, partner, pair)


def rows_kernel(ids, keep, partners, pair, own, later):
    c = ids[2]
    position = 2 * ids[1] + c
    total = keep[...] + partners[1 - c].astype(F32)
    place = lax.rem(iota((64, 2 * LANES), 1) // 32, 8)

    def finish(got):
        result = total + got
        own[...] = result[:, :LANES]
        later[...] = result[:, LANES:].astype(BF16)

    @pl.when((position > 0) & (position < 7))
    def _():
        finish(pair[...].astype(F32))

    @pl.when(position == 0)
    def _():
        finish(jnp.where(place == 0, 0.0, pltpu.roll(pair[...].astype(F32), 32, 1)))

    @pl.when(position == 7)
    def _():
        got = pltpu.roll(pair[...].astype(F32), 2 * LANES - 32, 1)
        finish(jnp.where(place == 7, 0.0, got))


def block_values(ids, own, earlier, bias):
    row = iota((64, CHANNELS), 0)
    wanted = BLOCK * ids[0] + 6 * (row // 8) + lax.rem(row, 8)
    chosen = (iota((64, CHANNELS), 1) == wanted) & (lax.rem(row, 8) < 6)
    biases = jnp.where(chosen, bias[...].reshape(1, CHANNELS), 0.0)
    column = jnp.sum(biases, axis=1, keepdims=True)
    total = (own[...] + earlier[...].astype(F32) + column).astype(BF16)
    to, frm = iota((BLOCK, 64), 0), iota((BLOCK, 64), 1)
    pick = (frm == 8 * (to // 6) + lax.rem(to, 6)).astype(BF16)
    return jnp.dot(pick, total, preferred_element_type=F32).astype(BF16)


def middle_kernel(ids, after, own, earlier, bias, middle):
    result = block_values(ids, own, earlier, bias)
    for z in range(8):
        middle[z] = result


def spread_kernel(ids, own, earlier, bias, latent, pieces, kept):
    result = block_values(ids, own, earlier, bias)
    for z in range(8):
        frames = [result[:, 256 * f + 32 * z : 256 * f + 32 * z + 32] for f in range(2)]
        pieces[z] = jnp.concatenate(frames, axis=1)
    kept[...] = latent[...]


def finish_kernel(latent, gathered, out):
    square = (CHANNELS, CHANNELS)
    same = iota(square, 0) == iota(square, 1)
    conv = lax.dot_general(
        gathered[...].reshape(CHANNELS, 64),
        same.astype(BF16),
        (((0,), (0,)), ((), ())),
        preferred_element_type=F32,
    )
    out[...] = (latent[...].astype(F32) + conv).astype(BF16)


def swap_cores(value):
    return lax.ppermute(value, "core", [(0, 1), (1, 0)])


def exchange(ids, keep, partner, pair):
    swaps = []
    for x in range(4):
        last, first = 2 * x + 1, 2 * ((x + 1) % 4)
        swaps += [(last, first), (first, last)]
    pair = lax.ppermute(pair, ("x", "core"), swaps)
    partners = lax.all_gather(partner, "core", axis=0)
    own, later = call(
        rows_kernel,
        [shape((64, LANES), F32), shape((64, LANES), BF16)],
        smem=1,
        n=4,
    )(ids, keep, partners, pair)
    return own, lax.ppermute(later, "t", [(i, i + 1) for i in range(7)])


def gather_weights(piece):
    one, two, three = [
        lax.ppermute(piece, "x", [(i, (i + by) % 4) for i in range(4)]) for by in (1, 2, 3)
    ]
    packed = jnp.stack([piece, one, two, three])
    return (piece, one, three, two), packed


def per_device(latent, gain_one, weight_one, bias_one, gain_two, weight_two, bias_two):
    ids = jnp.stack([lax.axis_index(a) for a in ("z", "x", "core")]).astype(jnp.int32)
    latent = latent.reshape(64, CHANNELS)
    weight_one, weight_two = [
        jnp.transpose(w, (0, 1, 2, 4, 3)).reshape(27, 6, CHANNELS)
        for w in (weight_one, weight_two)
    ]
    piece = shape((PIECE, CHANNELS), BF16)
    sums = [
        shape((64, 2 * LANES), F32),
        shape((64, 2 * LANES), BF16),
        shape((64, 2 * LANES), BF16),
    ]
    whole = pltpu.VMEM((8, SLOT, CHANNELS), BF16)
    products = pltpu.VMEM((8 * SLOT, LANES), F32)

    hidden = call(norm_kernel, shape((8, 64, CHANNELS), BF16), n=2)(latent, gain_one)
    pieces = call(prepare_kernel, [piece, piece], [pltpu.VMEM((PIECE, CHANNELS), F32)], n=2)(
        weight_one, weight_two
    )
    (weights_one, packed_one), (weights_two, packed_two) = [gather_weights(p) for p in pieces]
    gathered = lax.all_to_all(hidden, "z", 0, 0)
    sums_one = call(
        conv_one_kernel,
        sums,
        [whole, pltpu.VMEM((LANES, CHANNELS), BF16), products],
        smem=1,
        n=7,
    )(ids, gathered, *weights_one, swap_cores(packed_one))
    own, earlier = exchange(ids, *sums_one)
    middle = call(middle_kernel, shape((8, BLOCK, LANES), BF16), smem=1, anywhere=1, n=5)(
        ids, packed_two, own, earlier, bias_one
    )
    gathered = lax.all_to_all(middle, "z", 0, 0)
    sums_two = call(conv_two_kernel, sums, [whole, products], smem=1, n=8)(
        ids, gathered, gain_two, *weights_two, swap_cores(packed_two)
    )
    own, earlier = exchange(ids, *sums_two)
    pieces, kept = call(
        spread_kernel,
        [shape((8, BLOCK, 64), BF16), shape((64, CHANNELS), BF16)],
        smem=1,
        n=5,
    )(ids, own, earlier, bias_two, latent)
    pieces = lax.all_to_all(pieces, "z", 0, 0)
    out = call(finish_kernel, shape((64, CHANNELS), BF16), n=2)(kept, pieces)
    return out.reshape(2, 1, 32, CHANNELS)


def solution(mesh):
    mesh = Mesh(mesh.devices.reshape(8, 8, 4, 2), ("t", "z", "x", "core"))
    rows = ("z", "x", "core")
    kernel = P(None, None, None, None, rows)
    field = P("t", rows, None, None)
    return jax.shard_map(
        per_device,
        mesh=mesh,
        in_specs=(field, P(), kernel, P(), P(), kernel, P()),
        out_specs=field,
        check_vma=False,
    )
```

```python
import jax
import jax.numpy as jnp
from jax import lax
from jax.experimental import pallas as pl
from jax.experimental.pallas import tpu as pltpu
from jax.sharding import Mesh
from jax.sharding import PartitionSpec as P

CHANNELS = 384
BLOCK = 48
SLOT = 224
LANES = 512
VMEM = 48 * 1024 * 1024
F32 = jnp.float32
BF16 = jnp.bfloat16


def call(kernel, out_shape, scratch=(), smem=0, hbm=0, anywhere=0, n=0, vmem_limit=VMEM):
    specs = [pl.BlockSpec(memory_space=pltpu.SMEM)] * smem
    specs += [pl.BlockSpec(memory_space=pltpu.HBM)] * hbm
    specs += [pl.BlockSpec(memory_space=pl.ANY)] * anywhere
    specs += [pl.BlockSpec(memory_space=pltpu.VMEM)] * (n - len(specs))
    multiple = isinstance(out_shape, (list, tuple))
    vmem = pl.BlockSpec(memory_space=pltpu.VMEM)
    return pl.pallas_call(
        kernel,
        out_shape=out_shape,
        in_specs=specs,
        out_specs=[vmem] * len(out_shape) if multiple else vmem,
        scratch_shapes=list(scratch),
        compiler_params=pltpu.CompilerParams(vmem_limit_bytes=vmem_limit),
    )


def shape(dims, dtype):
    return jax.ShapeDtypeStruct(dims, dtype)


def iota(dims, axis):
    return lax.broadcasted_iota(jnp.int32, dims, axis)


def silu(v):
    return v / (1.0 + jnp.exp(-v))


def first_kernel(
    latent_hbm, one_hbm, two_hbm, gain_hbm, hidden, piece_one, piece_two, pieces, latent, gain, weights, rows, sems
):
    copies = [
        pltpu.make_async_copy(one_hbm, weights.at[0], sems.at[0]),
        pltpu.make_async_copy(two_hbm, weights.at[1], sems.at[1]),
        pltpu.make_async_copy(latent_hbm, latent, sems.at[2]),
        pltpu.make_async_copy(gain_hbm, gain, sems.at[3]),
    ]
    for copy in copies:
        copy.start()
    rows[...] = jnp.zeros_like(rows)
    for conv, piece in enumerate((piece_one, piece_two)):
        copies[conv].wait()
        for tap in range(27):
            rows[8 * tap : 8 * tap + 6, :] = weights[conv, tap].astype(F32)
        packed = rows[...].astype(BF16)
        piece[...] = packed
        pieces[conv] = packed
    copies[2].wait()
    copies[3].wait()
    values = latent[...].astype(F32)
    mean = jnp.mean(values * values, axis=1, keepdims=True)
    scale = lax.rsqrt(mean + 1e-6) * gain[...].reshape(1, CHANNELS)
    result = silu(values * scale).astype(BF16)
    for z in range(8):
        hidden[z] = result


def place_weights(conv, ids, both, near, far, swapped, whole):
    x, c = ids[1], ids[2]

    def place(position, value):
        whole[position] = value

    chip = jnp.bitwise_xor(x, 1 + 2 * c)
    other = jnp.bitwise_xor(x, 3 - 2 * c)
    across = jnp.bitwise_xor(x, 2)
    for i in range(2):
        place(2 * x + i, both[i])
        place(2 * chip + i, near[i])
        place(2 * other + i, swapped[i])
    place(2 * across + c, far[conv])
    place(2 * across + 1 - c, swapped[2])


def taps(ids, products, keep, partner, pair):
    c = ids[2]
    column = lax.rem(iota((8, 2 * LANES), 1), 32)
    half = LANES // 2
    for two in range(4):
        parts = ([], [], [])
        for slot in (2 * two, 2 * two + 1):
            for j in range(3):
                sums = []
                for l in range(3):
                    k = [
                        products[pl.ds(slot * SLOT + 8 * (9 * i + 3 * j + l), 8), :]
                        for i in range(3)
                    ]
                    frames = [
                        k[2][:, :half],
                        k[2][:, half:] + k[1][:, :half],
                        k[1][:, half:] + k[0][:, :half],
                        k[0][:, half:],
                    ]
                    sums.append(jnp.concatenate(frames, axis=1))
                left = jnp.where(column == 0, 0.0, pltpu.roll(sums[0], 1, 1))
                right = jnp.where(column == 31, 0.0, pltpu.roll(sums[2], 2 * LANES - 1, 1))
                parts[j].append(sums[1] + left + right)
        below, level, above = [jnp.concatenate(p, axis=0) for p in parts]
        at = pl.ds(16 * two, 16)
        keep[at, :] = level
        partner[at, :] = jnp.where(c == 0, below, above).astype(BF16)
        pair[at, :] = jnp.where(c == 0, above, below).astype(BF16)


def conv_one_kernel(ids, gathered, *rest):
    *pieces, keep, partner, pair, whole, field, products = rest
    place_weights(0, ids, *pieces, whole)
    for z in range(8):
        for f in range(2):
            field[pl.ds(256 * f + 32 * z, 32), :] = gathered[z, pl.ds(32 * f, 32), :]
    products[...] = lax.dot_general(
        whole[...].reshape(8 * SLOT, CHANNELS),
        field[...],
        (((1,), (1,)), ((), ())),
        preferred_element_type=F32,
    )
    taps(ids, products, keep, partner, pair)


def conv_two_kernel(ids, gathered, gain, *rest):
    *pieces, keep, partner, pair, whole, products = rest
    place_weights(1, ids, *pieces, whole)
    values = gathered[...].reshape(CHANNELS, LANES).astype(F32)
    mean = jnp.mean(values * values, axis=0, keepdims=True)
    square = (CHANNELS, CHANNELS)
    same = iota(square, 0) == iota(square, 1)
    gains = jnp.where(same, gain[...].reshape(1, CHANNELS), 0.0)
    scale = jnp.sum(gains, axis=1, keepdims=True)
    field = silu(values * lax.rsqrt(mean + 1e-6) * scale).astype(BF16)
    products[...] = jnp.dot(
        whole[...].reshape(8 * SLOT, CHANNELS), field, preferred_element_type=F32
    )
    taps(ids, products, keep, partner, pair)


def rows_kernel(ids, keep, partners, pair, own, later):
    c = ids[2]
    position = 2 * ids[1] + c
    total = keep[...] + partners[1 - c].astype(F32)
    place = lax.rem(iota((64, 2 * LANES), 1) // 32, 8)

    def finish(got):
        result = total + got
        own[...] = result[:, :LANES]
        later[...] = result[:, LANES:].astype(BF16)

    @pl.when((position > 0) & (position < 7))
    def _():
        finish(pair[...].astype(F32))

    @pl.when(position == 0)
    def _():
        finish(jnp.where(place == 0, 0.0, pltpu.roll(pair[...].astype(F32), 32, 1)))

    @pl.when(position == 7)
    def _():
        got = pltpu.roll(pair[...].astype(F32), 2 * LANES - 32, 1)
        finish(jnp.where(place == 7, 0.0, got))


def block_values(ids, own, earlier, bias):
    row = iota((64, CHANNELS), 0)
    wanted = BLOCK * ids[0] + 6 * (row // 8) + lax.rem(row, 8)
    chosen = (iota((64, CHANNELS), 1) == wanted) & (lax.rem(row, 8) < 6)
    biases = jnp.where(chosen, bias[...].reshape(1, CHANNELS), 0.0)
    column = jnp.sum(biases, axis=1, keepdims=True)
    total = (own[...] + earlier[...].astype(F32) + column).astype(BF16)
    to, frm = iota((BLOCK, 64), 0), iota((BLOCK, 64), 1)
    pick = (frm == 8 * (to // 6) + lax.rem(to, 6)).astype(BF16)
    return jnp.dot(pick, total, preferred_element_type=F32).astype(BF16)


def middle_kernel(ids, after, own, earlier, bias, middle):
    result = block_values(ids, own, earlier, bias)
    for z in range(8):
        middle[z] = result


def spread_kernel(ids, own, earlier, bias, latent, pieces, kept):
    result = block_values(ids, own, earlier, bias)
    result = result.astype(F32)
    for z in range(8):
        parts = []
        for first in (0, 24):
            for f in range(2):
                at = 256 * f + 32 * z
                parts.append(result[first : first + 24, at : at + 32])
        pieces[z] = jnp.concatenate(parts, axis=1).astype(BF16)
    kept[...] = latent[...]


def finish_kernel(latent, gathered, out):
    halves = gathered[...].reshape(8 * 24, 128)
    frm, to = iota((8 * 24, CHANNELS), 0), iota((8 * 24, CHANNELS), 1)
    conv = jnp.zeros((64, CHANNELS), F32)
    for half in range(2):
        pick = (to == BLOCK * (frm // 24) + lax.rem(frm, 24) + 24 * half).astype(F32).astype(BF16)
        conv += lax.dot_general(
            halves[:, 64 * half : 64 * half + 64],
            pick,
            (((0,), (0,)), ((), ())),
            preferred_element_type=F32,
        )
    out[...] = (latent[...].astype(F32) + conv).astype(BF16)


def swap_cores(value):
    return lax.ppermute(value, "core", [(0, 1), (1, 0)])


def exchange(ids, keep, partner, pair):
    swaps = []
    for x in range(4):
        last, first = 2 * x + 1, 2 * ((x + 1) % 4)
        swaps += [(last, first), (first, last)]
    pair = lax.ppermute(pair, ("x", "core"), swaps)
    partners = lax.all_gather(partner, "core", axis=0)
    own, later = call(
        rows_kernel,
        [shape((64, LANES), F32), shape((64, LANES), BF16)],
        smem=1,
        n=4,
    )(ids, keep, partners, pair)
    return own, lax.ppermute(later, "t", [(i, i + 1) for i in range(7)])


def gather_weights(piece_one, piece_two, pieces):
    hops = []
    for x in range(4):
        hops += [(2 * x, 2 * (x ^ 1)), (2 * x + 1, 2 * (x ^ 3) + 1)]
    far = lax.ppermute(pieces, "x", [(x, x ^ 2) for x in range(4)])
    result = []
    for conv, piece in enumerate((piece_one, piece_two)):
        both = lax.all_gather(piece, "core", axis=0)
        near = lax.ppermute(both, ("x", "core"), hops)
        result.append(((both, near, far), jnp.concatenate([near, far[conv : conv + 1]])))
    return result


def per_device(latent, gain_one, weight_one, bias_one, gain_two, weight_two, bias_two):
    ids = jnp.stack([lax.axis_index(a) for a in ("z", "x", "core")]).astype(jnp.int32)
    latent = latent.reshape(64, CHANNELS)
    weight_one, weight_two = [
        jnp.transpose(w, (0, 1, 2, 4, 3)).reshape(27, 6, CHANNELS)
        for w in (weight_one, weight_two)
    ]
    piece = shape((SLOT, CHANNELS), BF16)
    sums = [
        shape((64, 2 * LANES), F32),
        shape((64, 2 * LANES), BF16),
        shape((64, 2 * LANES), BF16),
    ]
    whole = pltpu.VMEM((8, SLOT, CHANNELS), BF16)
    products = pltpu.VMEM((8 * SLOT, LANES), F32)

    hidden, *pieces = call(
        first_kernel,
        [
            shape((8, 64, CHANNELS), BF16),
            piece,
            piece,
            shape((2, SLOT, CHANNELS), BF16),
        ],
        [
            pltpu.VMEM((64, CHANNELS), BF16),
            pltpu.VMEM((CHANNELS,), F32),
            pltpu.VMEM((2, 27, 6, CHANNELS), BF16),
            pltpu.VMEM((SLOT, CHANNELS), F32),
            pltpu.SemaphoreType.DMA((4,)),
        ],
        hbm=4,
        n=4,
        vmem_limit=60 * 1024 * 1024,
    )(latent, weight_one, weight_two, gain_one)
    (weights_one, packed_one), (weights_two, packed_two) = gather_weights(*pieces)
    gathered = lax.all_to_all(hidden, "z", 0, 0)
    sums_one = call(
        conv_one_kernel,
        sums,
        [whole, pltpu.VMEM((LANES, CHANNELS), BF16), products],
        smem=1,
        n=6,
    )(ids, gathered, *weights_one, swap_cores(packed_one))
    own, earlier = exchange(ids, *sums_one)
    middle = call(middle_kernel, shape((8, BLOCK, LANES), BF16), smem=1, anywhere=1, n=5)(
        ids, packed_two, own, earlier, bias_one
    )
    gathered = lax.all_to_all(middle, "z", 0, 0)
    sums_two = call(conv_two_kernel, sums, [whole, products], smem=1, n=7)(
        ids, gathered, gain_two, *weights_two, swap_cores(packed_two)
    )
    own, earlier = exchange(ids, *sums_two)
    pieces, kept = call(
        spread_kernel,
        [shape((8, 24, 128), BF16), shape((64, CHANNELS), BF16)],
        smem=1,
        n=5,
    )(ids, own, earlier, bias_two, latent)
    pieces = lax.all_to_all(pieces, "z", 0, 0)
    out = call(finish_kernel, shape((64, CHANNELS), BF16), n=2)(kept, pieces)
    return out.reshape(2, 1, 32, CHANNELS)


def solution(mesh):
    mesh = Mesh(mesh.devices.reshape(8, 8, 4, 2), ("t", "z", "x", "core"))
    rows = ("z", "x", "core")
    kernel = P(None, None, None, None, rows)
    field = P("t", rows, None, None)
    return jax.shard_map(
        per_device,
        mesh=mesh,
        in_specs=(field, P(), kernel, P(), P(), kernel, P()),
        out_specs=field,
        check_vma=False,
    )
```

```python
import functools

import jax
import jax.numpy as jnp
from jax import lax
from jax.experimental import pallas as pl
from jax.experimental.pallas import tpu as pltpu
from jax.sharding import Mesh
from jax.sharding import PartitionSpec as P

CHANNELS = 384
BLOCK = 48
GROUP = 80
SLOT = 3 * GROUP
LANES = 512
VMEM = 48 * 1024 * 1024
F32 = jnp.float32
BF16 = jnp.bfloat16


def call(kernel, out_shape, scratch=(), smem=0, hbm=0, anywhere=0, n=0, vmem_limit=VMEM, flops=0):
    specs = [pl.BlockSpec(memory_space=pltpu.SMEM)] * smem
    specs += [pl.BlockSpec(memory_space=pltpu.HBM)] * hbm
    specs += [pl.BlockSpec(memory_space=pl.ANY)] * anywhere
    specs += [pl.BlockSpec(memory_space=pltpu.VMEM)] * (n - len(specs))
    multiple = isinstance(out_shape, (list, tuple))
    vmem = pl.BlockSpec(memory_space=pltpu.VMEM)
    return pl.pallas_call(
        kernel,
        out_shape=out_shape,
        in_specs=specs,
        out_specs=[vmem] * len(out_shape) if multiple else vmem,
        scratch_shapes=list(scratch),
        compiler_params=pltpu.CompilerParams(vmem_limit_bytes=vmem_limit),
        cost_estimate=pl.CostEstimate(flops=flops, bytes_accessed=0, transcendentals=0),
    )


def shape(dims, dtype):
    return jax.ShapeDtypeStruct(dims, dtype)


def iota(dims, axis):
    return lax.broadcasted_iota(jnp.int32, dims, axis)


def silu(v):
    return v / (1.0 + jnp.exp(-v))


def first_kernel(
    latent_hbm, one_hbm, two_hbm, gain_hbm, hidden, piece_one, piece_two, pieces, latent, gain, weights, rows, sems
):
    copies = [
        pltpu.make_async_copy(one_hbm, weights.at[0], sems.at[0]),
        pltpu.make_async_copy(two_hbm, weights.at[1], sems.at[1]),
        pltpu.make_async_copy(latent_hbm, latent, sems.at[2]),
        pltpu.make_async_copy(gain_hbm, gain, sems.at[3]),
    ]
    for copy in copies:
        copy.start()
    rows[...] = jnp.zeros_like(rows)
    for conv, piece in enumerate((piece_one, piece_two)):
        copies[conv].wait()
        for tap in range(27):
            at = GROUP * (tap // 3 % 3) + 8 * (3 * (tap // 9) + tap % 3)
            rows[at : at + 6, :] = weights[conv, tap].astype(F32)
        packed = rows[...].astype(BF16)
        piece[...] = packed
        pieces[conv] = packed
    copies[2].wait()
    copies[3].wait()
    values = latent[...].astype(F32)
    mean = jnp.mean(values * values, axis=1, keepdims=True)
    scale = lax.rsqrt(mean + 1e-6) * gain[...].reshape(1, CHANNELS)
    result = silu(values * scale).astype(BF16)
    for z in range(8):
        hidden[z] = result


def place_weights(conv, height, ids, both, near, far, swapped, group):
    x, c = ids[1], ids[2]
    chip = jnp.bitwise_xor(x, 1 + 2 * c)
    other = jnp.bitwise_xor(x, 3 - 2 * c)
    across = jnp.bitwise_xor(x, 2)
    rows = pl.ds(pl.multiple_of(GROUP * height, 16), GROUP)
    for i in range(2):
        group[2 * x + i] = both[i, rows, :]
        group[2 * chip + i] = near[i, rows, :]
        group[2 * other + i] = swapped[i, rows, :]
    group[2 * across + c] = far[conv, rows, :]
    group[2 * across + 1 - c] = swapped[2, rows, :]


def taps(products, first, emit):
    column = lax.rem(iota((8, 2 * LANES), 1), 32)
    half = LANES // 2
    for two in range(4):
        rows = []
        for slot in (2 * two, 2 * two + 1):
            sums = []
            for l in range(3):
                k = [products[pl.ds(first(slot) + 8 * (3 * i + l), 8), :] for i in range(3)]
                frames = [
                    k[2][:, :half],
                    k[2][:, half:] + k[1][:, :half],
                    k[1][:, half:] + k[0][:, :half],
                    k[0][:, half:],
                ]
                sums.append(jnp.concatenate(frames, axis=1))
            left = jnp.where(column == 0, 0.0, pltpu.roll(sums[0], 1, 1))
            right = jnp.where(column == 31, 0.0, pltpu.roll(sums[2], 2 * LANES - 1, 1))
            rows.append(sums[1] + left + right)
        emit(pl.ds(16 * two, 16), jnp.concatenate(rows, axis=0))


def multiply(axis, group, field):
    return lax.dot_general(
        group, field, (((1,), (axis,)), ((), ())), preferred_element_type=F32
    )


def pair_sums(conv, axis, ids, field, pieces, pair, group, products):
    place_weights(conv, 2 - 2 * ids[2], ids, *pieces, group)
    products[...] = multiply(axis, group[...].reshape(8 * GROUP, CHANNELS), field)

    def emit(at, value):
        pair[at, :] = value.astype(BF16)

    taps(products, lambda slot: slot * GROUP, emit)


def field_kernel(gathered, field):
    for z in range(8):
        for f in range(2):
            field[pl.ds(256 * f + 32 * z, 32), :] = gathered[z, pl.ds(32 * f, 32), :]


def pair_one_kernel(ids, field, *rest):
    *pieces, pair, group, products = rest
    pair_sums(0, 1, ids, field[...], pieces, pair, group, products)


def pair_two_kernel(ids, gathered, gain, *rest):
    *pieces, pair, field, group, products = rest
    values = gathered[...].reshape(CHANNELS, LANES).astype(F32)
    mean = jnp.mean(values * values, axis=0, keepdims=True)
    square = (CHANNELS, CHANNELS)
    same = iota(square, 0) == iota(square, 1)
    gains = jnp.where(same, gain[...].reshape(1, CHANNELS), 0.0)
    scale = jnp.sum(gains, axis=1, keepdims=True)
    hidden = silu(values * lax.rsqrt(mean + 1e-6) * scale).astype(BF16)
    field[...] = hidden
    pair_sums(1, 0, ids, hidden, pieces, pair, group, products)


def rest_kernel(conv, axis, ids, field, *rest):
    *pieces, keep, partner, groups, products = rest
    place_weights(conv, 1, ids, *pieces, groups.at[0])
    place_weights(conv, 2 * ids[2], ids, *pieces, groups.at[1])
    products[...] = multiply(axis, groups[...].reshape(16 * GROUP, CHANNELS), field[...])

    def emit_keep(at, value):
        keep[at, :] = value

    def emit_partner(at, value):
        partner[at, :] = value.astype(BF16)

    taps(products, lambda slot: (8 + slot) * GROUP, emit_partner)
    taps(products, lambda slot: slot * GROUP, emit_keep)


def rows_kernel(ids, keep, partners, pair, own, later):
    c = ids[2]
    position = 2 * ids[1] + c
    total = keep[...] + partners[1 - c].astype(F32)
    place = lax.rem(iota((64, 2 * LANES), 1) // 32, 8)

    def finish(got):
        result = total + got
        own[...] = result[:, :LANES]
        later[...] = result[:, LANES:].astype(BF16)

    @pl.when((position > 0) & (position < 7))
    def _():
        finish(pair[...].astype(F32))

    @pl.when(position == 0)
    def _():
        finish(jnp.where(place == 0, 0.0, pltpu.roll(pair[...].astype(F32), 32, 1)))

    @pl.when(position == 7)
    def _():
        got = pltpu.roll(pair[...].astype(F32), 2 * LANES - 32, 1)
        finish(jnp.where(place == 7, 0.0, got))


def block_values(ids, own, earlier, bias):
    row = iota((64, CHANNELS), 0)
    wanted = BLOCK * ids[0] + 6 * (row // 8) + lax.rem(row, 8)
    chosen = (iota((64, CHANNELS), 1) == wanted) & (lax.rem(row, 8) < 6)
    biases = jnp.where(chosen, bias[...].reshape(1, CHANNELS), 0.0)
    column = jnp.sum(biases, axis=1, keepdims=True)
    total = (own[...] + earlier[...].astype(F32) + column).astype(BF16)
    to, frm = iota((BLOCK, 64), 0), iota((BLOCK, 64), 1)
    pick = (frm == 8 * (to // 6) + lax.rem(to, 6)).astype(BF16)
    return jnp.dot(pick, total, preferred_element_type=F32).astype(BF16)


def middle_kernel(ids, after, own, earlier, bias, middle):
    result = block_values(ids, own, earlier, bias)
    for z in range(8):
        middle[z] = result


def spread_kernel(ids, own, earlier, bias, latent, pieces, kept):
    result = block_values(ids, own, earlier, bias)
    result = result.astype(F32)
    for z in range(8):
        parts = []
        for first in (0, 24):
            for f in range(2):
                at = 256 * f + 32 * z
                parts.append(result[first : first + 24, at : at + 32])
        pieces[z] = jnp.concatenate(parts, axis=1).astype(BF16)
    kept[...] = latent[...]


def finish_kernel(latent, gathered, out):
    halves = gathered[...].reshape(8 * 24, 128)
    frm, to = iota((8 * 24, CHANNELS), 0), iota((8 * 24, CHANNELS), 1)
    conv = jnp.zeros((64, CHANNELS), F32)
    for half in range(2):
        pick = (to == BLOCK * (frm // 24) + lax.rem(frm, 24) + 24 * half).astype(F32).astype(BF16)
        conv += lax.dot_general(
            halves[:, 64 * half : 64 * half + 64],
            pick,
            (((0,), (0,)), ((), ())),
            preferred_element_type=F32,
        )
    out[...] = (latent[...].astype(F32) + conv).astype(BF16)


def swap_cores(value):
    return lax.ppermute(value, "core", [(0, 1), (1, 0)])


def swap_chips(pair):
    swaps = []
    for x in range(4):
        last, first = 2 * x + 1, 2 * ((x + 1) % 4)
        swaps += [(last, first), (first, last)]
    return lax.ppermute(pair, ("x", "core"), swaps)


def exchange(ids, pair, keep, partner):
    partners = lax.all_gather(partner, "core", axis=0)
    own, later = call(
        rows_kernel,
        [shape((64, LANES), F32), shape((64, LANES), BF16)],
        smem=1,
        n=4,
    )(ids, keep, partners, pair)
    return own, lax.ppermute(later, "t", [(i, i + 1) for i in range(7)])


def gather_weights(piece_one, piece_two, pieces):
    hops = []
    for x in range(4):
        hops += [(2 * x, 2 * (x ^ 1)), (2 * x + 1, 2 * (x ^ 3) + 1)]
    far = lax.ppermute(pieces, "x", [(x, x ^ 2) for x in range(4)])
    result = []
    chip = lax.all_gather(pieces, "core", axis=1)
    for conv, piece in enumerate((piece_one, piece_two)):
        both = chip[conv]
        near = lax.ppermute(both, ("x", "core"), hops)
        result.append(((both, near, far), jnp.concatenate([near, far[conv : conv + 1]])))
    return result


def per_device(latent, gain_one, weight_one, bias_one, gain_two, weight_two, bias_two):
    ids = jnp.stack([lax.axis_index(a) for a in ("z", "x", "core")]).astype(jnp.int32)
    latent = latent.reshape(64, CHANNELS)
    weight_one, weight_two = [
        jnp.transpose(w, (0, 1, 2, 4, 3)).reshape(27, 6, CHANNELS)
        for w in (weight_one, weight_two)
    ]
    piece = shape((SLOT, CHANNELS), BF16)
    half = shape((64, 2 * LANES), BF16)
    sums = [shape((64, 2 * LANES), F32), half]
    group = pltpu.VMEM((8, GROUP, CHANNELS), BF16)
    groups = pltpu.VMEM((2, 8, GROUP, CHANNELS), BF16)
    products = pltpu.VMEM((8 * GROUP, LANES), F32)
    products_rest = pltpu.VMEM((16 * GROUP, LANES), F32)
    rest = lambda conv, axis: call(
        functools.partial(rest_kernel, conv, axis), sums, [groups, products_rest], smem=1, n=6
    )

    hidden, *pieces = call(
        first_kernel,
        [
            shape((8, 64, CHANNELS), BF16),
            piece,
            piece,
            shape((2, SLOT, CHANNELS), BF16),
        ],
        [
            pltpu.VMEM((64, CHANNELS), BF16),
            pltpu.VMEM((CHANNELS,), F32),
            pltpu.VMEM((2, 27, 6, CHANNELS), BF16),
            pltpu.VMEM((SLOT, CHANNELS), F32),
            pltpu.SemaphoreType.DMA((4,)),
        ],
        hbm=4,
        n=4,
        vmem_limit=60 * 1024 * 1024,
    )(latent, weight_one, weight_two, gain_one)
    (weights_one, packed_one), (weights_two, packed_two) = gather_weights(*pieces)
    gathered = lax.all_to_all(hidden, "z", 0, 0)
    field = call(field_kernel, shape((LANES, CHANNELS), BF16), n=1, flops=10**11)(gathered)
    weights_one += (swap_cores(packed_one),)
    pair = call(pair_one_kernel, half, [group, products], smem=1, n=6)(ids, field, *weights_one)
    own, earlier = exchange(ids, swap_chips(pair), *rest(0, 1)(ids, field, *weights_one))
    middle = call(middle_kernel, shape((8, BLOCK, LANES), BF16), smem=1, anywhere=1, n=5)(
        ids, packed_two, own, earlier, bias_one
    )
    gathered = lax.all_to_all(middle, "z", 0, 0)
    weights_two += (swap_cores(packed_two),)
    pair, field = call(
        pair_two_kernel,
        [half, shape((CHANNELS, LANES), BF16)],
        [group, products],
        smem=1,
        n=7,
    )(ids, gathered, gain_two, *weights_two)
    own, earlier = exchange(ids, swap_chips(pair), *rest(1, 0)(ids, field, *weights_two))
    pieces, kept = call(
        spread_kernel,
        [shape((8, 24, 128), BF16), shape((64, CHANNELS), BF16)],
        smem=1,
        n=5,
    )(ids, own, earlier, bias_two, latent)
    pieces = lax.all_to_all(pieces, "z", 0, 0)
    out = call(finish_kernel, shape((64, CHANNELS), BF16), n=2)(kept, pieces)
    return out.reshape(2, 1, 32, CHANNELS)


def solution(mesh):
    mesh = Mesh(mesh.devices.reshape(8, 8, 4, 2), ("t", "z", "x", "core"))
    rows = ("z", "x", "core")
    kernel = P(None, None, None, None, rows)
    field = P("t", rows, None, None)
    return jax.shard_map(
        per_device,
        mesh=mesh,
        in_specs=(field, P(), kernel, P(), P(), kernel, P()),
        out_specs=field,
        check_vma=False,
    )
```

```python
import functools

import jax
import jax.numpy as jnp
from jax import lax
from jax.experimental import pallas as pl
from jax.experimental.pallas import tpu as pltpu
from jax.sharding import Mesh
from jax.sharding import PartitionSpec as P

CHANNELS = 384
BLOCK = 48
GROUP = 80
SLOT = 3 * GROUP
LANES = 512
VMEM = 48 * 1024 * 1024
F32 = jnp.float32
BF16 = jnp.bfloat16


def call(kernel, out_shape, scratch=(), smem=0, hbm=0, anywhere=0, n=0, vmem_limit=VMEM, flops=0):
    specs = [pl.BlockSpec(memory_space=pltpu.SMEM)] * smem
    specs += [pl.BlockSpec(memory_space=pltpu.HBM)] * hbm
    specs += [pl.BlockSpec(memory_space=pl.ANY)] * anywhere
    specs += [pl.BlockSpec(memory_space=pltpu.VMEM)] * (n - len(specs))
    multiple = isinstance(out_shape, (list, tuple))
    vmem = pl.BlockSpec(memory_space=pltpu.VMEM)
    return pl.pallas_call(
        kernel,
        out_shape=out_shape,
        in_specs=specs,
        out_specs=[vmem] * len(out_shape) if multiple else vmem,
        scratch_shapes=list(scratch),
        compiler_params=pltpu.CompilerParams(vmem_limit_bytes=vmem_limit),
        cost_estimate=pl.CostEstimate(flops=flops, bytes_accessed=0, transcendentals=0),
    )


def shape(dims, dtype):
    return jax.ShapeDtypeStruct(dims, dtype)


def iota(dims, axis):
    return lax.broadcasted_iota(jnp.int32, dims, axis)


def silu(v):
    return v / (1.0 + jnp.exp(-v))


def first_kernel(
    latent_hbm, one_hbm, two_hbm, gain_hbm, hidden, pieces, latent, gain, weights, rows, sems
):
    copies = [
        pltpu.make_async_copy(one_hbm, weights.at[0], sems.at[0]),
        pltpu.make_async_copy(two_hbm, weights.at[1], sems.at[1]),
        pltpu.make_async_copy(latent_hbm, latent, sems.at[2]),
        pltpu.make_async_copy(gain_hbm, gain, sems.at[3]),
    ]
    for copy in copies:
        copy.start()
    rows[...] = jnp.zeros_like(rows)
    for conv in range(2):
        copies[conv].wait()
        for tap in range(27):
            at = GROUP * (tap // 3 % 3) + 8 * (3 * (tap // 9) + tap % 3)
            rows[at : at + 6, :] = weights[conv, tap].astype(F32)
        pieces[conv] = rows[...].astype(BF16)
    copies[2].wait()
    copies[3].wait()
    values = latent[...].astype(F32)
    mean = jnp.mean(values * values, axis=1, keepdims=True)
    scale = lax.rsqrt(mean + 1e-6) * gain[...].reshape(1, CHANNELS)
    result = silu(values * scale).astype(BF16)
    for z in range(8):
        hidden[z] = result


def place_weights(conv, height, ids, both, near, far, other, group):
    x, c = ids[1], ids[2]
    across = jnp.bitwise_xor(x, 2)
    rows = pl.ds(pl.multiple_of(GROUP * height, 16), GROUP)
    for i in range(2):
        group[2 * x + i] = both[i, rows, :]
        group[2 * jnp.bitwise_xor(x, 1) + i] = near[0, i, rows, :]
        group[2 * jnp.bitwise_xor(x, 3) + i] = near[1, i, rows, :]
    group[2 * across + c] = far[conv, rows, :]
    group[2 * across + 1 - c] = other[conv, rows, :]


def taps(products, first, emit):
    column = lax.rem(iota((8, 2 * LANES), 1), 32)
    half = LANES // 2
    for two in range(4):
        rows = []
        for slot in (2 * two, 2 * two + 1):
            sums = []
            for l in range(3):
                k = [products[pl.ds(first(slot) + 8 * (3 * i + l), 8), :] for i in range(3)]
                frames = [
                    k[2][:, :half],
                    k[2][:, half:] + k[1][:, :half],
                    k[1][:, half:] + k[0][:, :half],
                    k[0][:, half:],
                ]
                sums.append(jnp.concatenate(frames, axis=1))
            left = jnp.where(column == 0, 0.0, pltpu.roll(sums[0], 1, 1))
            right = jnp.where(column == 31, 0.0, pltpu.roll(sums[2], 2 * LANES - 1, 1))
            rows.append(sums[1] + left + right)
        emit(pl.ds(16 * two, 16), jnp.concatenate(rows, axis=0))


def multiply(axis, group, field):
    return lax.dot_general(
        group, field, (((1,), (axis,)), ((), ())), preferred_element_type=F32
    )


def pair_sums(conv, axis, ids, field, pieces, pair, group, products):
    place_weights(conv, 2 - 2 * ids[2], ids, *pieces, group)
    products[...] = multiply(axis, group[...].reshape(8 * GROUP, CHANNELS), field)

    def emit(at, value):
        pair[at, :] = value.astype(BF16)

    taps(products, lambda slot: slot * GROUP, emit)


def field_kernel(gathered, field):
    for z in range(8):
        for f in range(2):
            field[pl.ds(256 * f + 32 * z, 32), :] = gathered[z, pl.ds(32 * f, 32), :]


def pair_one_kernel(ids, field, *rest):
    *pieces, pair, group, products = rest
    pair_sums(0, 1, ids, field[...], pieces, pair, group, products)


def pair_two_kernel(ids, gathered, gain, *rest):
    *pieces, pair, field, group, products = rest
    values = gathered[...].reshape(CHANNELS, LANES).astype(F32)
    mean = jnp.mean(values * values, axis=0, keepdims=True)
    square = (CHANNELS, CHANNELS)
    same = iota(square, 0) == iota(square, 1)
    gains = jnp.where(same, gain[...].reshape(1, CHANNELS), 0.0)
    scale = jnp.sum(gains, axis=1, keepdims=True)
    hidden = silu(values * lax.rsqrt(mean + 1e-6) * scale).astype(BF16)
    field[...] = hidden
    pair_sums(1, 0, ids, hidden, pieces, pair, group, products)


def rest_kernel(conv, axis, ids, field, *rest):
    *pieces, keep, partner, groups, products = rest
    place_weights(conv, 1, ids, *pieces, groups.at[0])
    place_weights(conv, 2 * ids[2], ids, *pieces, groups.at[1])
    products[...] = multiply(axis, groups[...].reshape(16 * GROUP, CHANNELS), field[...])

    def emit_keep(at, value):
        keep[at, :] = value

    def emit_partner(at, value):
        partner[at, :] = value.astype(BF16)

    taps(products, lambda slot: (8 + slot) * GROUP, emit_partner)
    taps(products, lambda slot: slot * GROUP, emit_keep)


def rows_kernel(ids, keep, partners, pair, bias, own, later):
    c = ids[2]
    position = 2 * ids[1] + c
    total = keep[...] + partners[1 - c].astype(F32)
    row = iota((64, CHANNELS), 0)
    wanted = BLOCK * ids[0] + 6 * (row // 8) + lax.rem(row, 8)
    chosen = (iota((64, CHANNELS), 1) == wanted) & (lax.rem(row, 8) < 6)
    biases = jnp.where(chosen, bias[...].reshape(1, CHANNELS), 0.0)
    column = jnp.sum(biases, axis=1, keepdims=True)
    place = lax.rem(iota((64, 2 * LANES), 1) // 32, 8)

    def finish(got):
        result = total + got
        own[...] = result[:, :LANES] + column
        later[...] = result[:, LANES:].astype(BF16)

    @pl.when((position > 0) & (position < 7))
    def _():
        finish(pair[...].astype(F32))

    @pl.when(position == 0)
    def _():
        finish(jnp.where(place == 0, 0.0, pltpu.roll(pair[...].astype(F32), 32, 1)))

    @pl.when(position == 7)
    def _():
        got = pltpu.roll(pair[...].astype(F32), 2 * LANES - 32, 1)
        finish(jnp.where(place == 7, 0.0, got))


def block_values(own, earlier):
    total = (own[...] + earlier[...].astype(F32)).astype(BF16)
    to, frm = iota((BLOCK, 64), 0), iota((BLOCK, 64), 1)
    pick = (frm == 8 * (to // 6) + lax.rem(to, 6)).astype(BF16)
    return jnp.dot(pick, total, preferred_element_type=F32).astype(BF16)


def middle_kernel(after, own, earlier, middle):
    result = block_values(own, earlier)
    for z in range(8):
        middle[z] = result


def spread_kernel(own, earlier, latent, pieces, kept):
    result = block_values(own, earlier)
    result = result.astype(F32)
    for z in range(8):
        parts = []
        for first in (0, 24):
            for f in range(2):
                at = 256 * f + 32 * z
                parts.append(result[first : first + 24, at : at + 32])
        pieces[z] = jnp.concatenate(parts, axis=1).astype(BF16)
    kept[...] = latent[...]


def finish_kernel(latent, gathered, out):
    halves = gathered[...].reshape(8 * 24, 128)
    frm, to = iota((8 * 24, CHANNELS), 0), iota((8 * 24, CHANNELS), 1)
    conv = jnp.zeros((64, CHANNELS), F32)
    for half in range(2):
        pick = (to == BLOCK * (frm // 24) + lax.rem(frm, 24) + 24 * half).astype(F32).astype(BF16)
        conv += lax.dot_general(
            halves[:, 64 * half : 64 * half + 64],
            pick,
            (((0,), (0,)), ((), ())),
            preferred_element_type=F32,
        )
    out[...] = (latent[...].astype(F32) + conv).astype(BF16)


def swap_cores(value):
    return lax.ppermute(value, "core", [(0, 1), (1, 0)])


def swap_chips(pair):
    swaps = []
    for x in range(4):
        last, first = 2 * x + 1, 2 * ((x + 1) % 4)
        swaps += [(last, first), (first, last)]
    return lax.ppermute(pair, ("x", "core"), swaps)


def exchange(ids, bias, pair, keep, partner):
    partners = lax.all_gather(partner, "core", axis=0)
    own, later = call(
        rows_kernel,
        [shape((64, LANES), F32), shape((64, LANES), BF16)],
        smem=1,
        n=5,
    )(ids, keep, partners, pair, bias)
    return own, lax.ppermute(later, "t", [(i, i + 1) for i in range(7)])


def gather_weights(pieces):
    hops = []
    for x in range(4):
        hops += [(2 * x, 2 * (x ^ 1)), (2 * x + 1, 2 * (x ^ 3) + 1)]
    far = lax.ppermute(pieces, "x", [(x, x ^ 2) for x in range(4)])
    other = swap_cores(far)
    chip = lax.all_gather(pieces, "core", axis=1)
    result = []
    for both in (chip[0], chip[1]):
        near = lax.all_gather(lax.ppermute(both, ("x", "core"), hops), "core", axis=0)
        result.append((both, near, far, other))
    return result


def per_device(latent, gain_one, weight_one, bias_one, gain_two, weight_two, bias_two):
    ids = jnp.stack([lax.axis_index(a) for a in ("z", "x", "core")]).astype(jnp.int32)
    latent = latent.reshape(64, CHANNELS)
    weight_one, weight_two = [
        jnp.transpose(w, (0, 1, 2, 4, 3)).reshape(27, 6, CHANNELS)
        for w in (weight_one, weight_two)
    ]
    half = shape((64, 2 * LANES), BF16)
    sums = [shape((64, 2 * LANES), F32), half]
    group = pltpu.VMEM((8, GROUP, CHANNELS), BF16)
    groups = pltpu.VMEM((2, 8, GROUP, CHANNELS), BF16)
    products = pltpu.VMEM((8 * GROUP, LANES), F32)
    products_rest = pltpu.VMEM((16 * GROUP, LANES), F32)
    rest = lambda conv, axis: call(
        functools.partial(rest_kernel, conv, axis), sums, [groups, products_rest], smem=1, n=6
    )

    hidden, pieces = call(
        first_kernel,
        [
            shape((8, 64, CHANNELS), BF16),
            shape((2, SLOT, CHANNELS), BF16),
        ],
        [
            pltpu.VMEM((64, CHANNELS), BF16),
            pltpu.VMEM((CHANNELS,), F32),
            pltpu.VMEM((2, 27, 6, CHANNELS), BF16),
            pltpu.VMEM((SLOT, CHANNELS), F32),
            pltpu.SemaphoreType.DMA((4,)),
        ],
        hbm=4,
        n=4,
        vmem_limit=60 * 1024 * 1024,
    )(latent, weight_one, weight_two, gain_one)
    weights_one, weights_two = gather_weights(pieces)
    gathered = lax.all_to_all(hidden, "z", 0, 0)
    field = call(field_kernel, shape((LANES, CHANNELS), BF16), n=1, flops=10**11)(gathered)
    pair = call(pair_one_kernel, half, [group, products], smem=1, n=6)(ids, field, *weights_one)
    own, earlier = exchange(ids, bias_one, swap_chips(pair), *rest(0, 1)(ids, field, *weights_one))
    middle = call(middle_kernel, shape((8, BLOCK, LANES), BF16), anywhere=1, n=3)(
        weights_two[1], own, earlier
    )
    gathered = lax.all_to_all(middle, "z", 0, 0)
    pair, field = call(
        pair_two_kernel,
        [half, shape((CHANNELS, LANES), BF16)],
        [group, products],
        smem=1,
        n=7,
    )(ids, gathered, gain_two, *weights_two)
    own, earlier = exchange(ids, bias_two, swap_chips(pair), *rest(1, 0)(ids, field, *weights_two))
    pieces, kept = call(
        spread_kernel,
        [shape((8, 24, 128), BF16), shape((64, CHANNELS), BF16)],
        n=3,
    )(own, earlier, latent)
    pieces = lax.all_to_all(pieces, "z", 0, 0)
    out = call(finish_kernel, shape((64, CHANNELS), BF16), n=2)(kept, pieces)
    return out.reshape(2, 1, 32, CHANNELS)


def solution(mesh):
    mesh = Mesh(mesh.devices.reshape(8, 8, 4, 2), ("t", "z", "x", "core"))
    rows = ("z", "x", "core")
    kernel = P(None, None, None, None, rows)
    field = P("t", rows, None, None)
    return jax.shard_map(
        per_device,
        mesh=mesh,
        in_specs=(field, P(), kernel, P(), P(), kernel, P()),
        out_specs=field,
        check_vma=False,
    )
```

```python
import functools

import jax
import jax.numpy as jnp
from jax import lax
from jax.experimental import pallas as pl
from jax.experimental.pallas import tpu as pltpu
from jax.sharding import Mesh
from jax.sharding import PartitionSpec as P

CHANNELS = 384
BLOCK = 48
GROUP = 80
SLOT = 3 * GROUP
LANES = 512
VMEM = 48 * 1024 * 1024
F32 = jnp.float32
BF16 = jnp.bfloat16


def call(kernel, out_shape, scratch=(), smem=0, hbm=0, anywhere=0, n=0, vmem_limit=VMEM, flops=0):
    specs = [pl.BlockSpec(memory_space=pltpu.SMEM)] * smem
    specs += [pl.BlockSpec(memory_space=pltpu.HBM)] * hbm
    specs += [pl.BlockSpec(memory_space=pl.ANY)] * anywhere
    specs += [pl.BlockSpec(memory_space=pltpu.VMEM)] * (n - len(specs))
    multiple = isinstance(out_shape, (list, tuple))
    vmem = pl.BlockSpec(memory_space=pltpu.VMEM)
    return pl.pallas_call(
        kernel,
        out_shape=out_shape,
        in_specs=specs,
        out_specs=[vmem] * len(out_shape) if multiple else vmem,
        scratch_shapes=list(scratch),
        compiler_params=pltpu.CompilerParams(vmem_limit_bytes=vmem_limit),
        cost_estimate=pl.CostEstimate(flops=flops, bytes_accessed=0, transcendentals=0),
    )


def shape(dims, dtype):
    return jax.ShapeDtypeStruct(dims, dtype)


def iota(dims, axis):
    return lax.broadcasted_iota(jnp.int32, dims, axis)


def silu(v):
    return v / (1.0 + jnp.exp(-v))


def first_kernel(
    latent_hbm, one_hbm, two_hbm, gain_hbm, hidden, pieces, latent, gain, weights, rows, sems
):
    copies = [
        pltpu.make_async_copy(one_hbm, weights.at[0], sems.at[0]),
        pltpu.make_async_copy(two_hbm, weights.at[1], sems.at[1]),
        pltpu.make_async_copy(latent_hbm, latent, sems.at[2]),
        pltpu.make_async_copy(gain_hbm, gain, sems.at[3]),
    ]
    for copy in copies:
        copy.start()
    rows[...] = jnp.zeros_like(rows)
    for conv in range(2):
        copies[conv].wait()
        for tap in range(27):
            at = GROUP * (tap // 3 % 3) + 8 * (3 * (tap // 9) + tap % 3)
            rows[at : at + 6, :] = weights[conv, tap].astype(F32)
        pieces[conv] = rows[...].astype(BF16)
    copies[2].wait()
    copies[3].wait()
    values = latent[...].astype(F32)
    mean = jnp.mean(values * values, axis=1, keepdims=True)
    scale = lax.rsqrt(mean + 1e-6) * gain[...].reshape(1, CHANNELS)
    result = silu(values * scale).astype(BF16)
    for z in range(8):
        hidden[z] = result


def place_weights(conv, height, ids, both, near, far, other, group):
    x, c = ids[1], ids[2]
    across = jnp.bitwise_xor(x, 2)
    rows = pl.ds(pl.multiple_of(GROUP * height, 16), GROUP)
    for i in range(2):
        group[2 * x + i] = both[i, rows, :]
        group[2 * jnp.bitwise_xor(x, 1) + i] = near[0, i, rows, :]
        group[2 * jnp.bitwise_xor(x, 3) + i] = near[1, i, rows, :]
    group[2 * across + c] = far[conv, rows, :]
    group[2 * across + 1 - c] = other[conv, rows, :]


def taps(products, first, emit):
    column = lax.rem(iota((8, 2 * LANES), 1), 32)
    half = LANES // 2
    for two in range(4):
        rows = []
        for slot in (2 * two, 2 * two + 1):
            sums = []
            for l in range(3):
                k = [products[pl.ds(first(slot) + 8 * (3 * i + l), 8), :] for i in range(3)]
                frames = [
                    k[2][:, :half],
                    k[2][:, half:] + k[1][:, :half],
                    k[1][:, half:] + k[0][:, :half],
                    k[0][:, half:],
                ]
                sums.append(jnp.concatenate(frames, axis=1))
            left = jnp.where(column == 0, 0.0, pltpu.roll(sums[0], 1, 1))
            right = jnp.where(column == 31, 0.0, pltpu.roll(sums[2], 2 * LANES - 1, 1))
            rows.append(sums[1] + left + right)
        emit(pl.ds(16 * two, 16), jnp.concatenate(rows, axis=0))


def multiply(axis, group, field):
    return lax.dot_general(
        group, field, (((1,), (axis,)), ((), ())), preferred_element_type=F32
    )


def pair_sums(conv, axis, ids, field, pieces, pair, group, products):
    place_weights(conv, 2 - 2 * ids[2], ids, *pieces, group)
    products[...] = multiply(axis, group[...].reshape(8 * GROUP, CHANNELS), field)

    def emit(at, value):
        pair[at, :] = value.astype(BF16)

    taps(products, lambda slot: slot * GROUP, emit)


def field_kernel(gathered, bias, field, kept):
    kept[...] = bias[...]
    for z in range(8):
        for f in range(2):
            field[pl.ds(256 * f + 32 * z, 32), :] = gathered[z, pl.ds(32 * f, 32), :]


def pair_one_kernel(ids, field, *rest):
    *pieces, pair, group, products = rest
    pair_sums(0, 1, ids, field[...], pieces, pair, group, products)


def pair_two_kernel(ids, gathered, gain, bias, *rest):
    *pieces, pair, field, kept, group, products = rest
    kept[...] = bias[...]
    values = gathered[...].reshape(CHANNELS, LANES).astype(F32)
    mean = jnp.mean(values * values, axis=0, keepdims=True)
    square = (CHANNELS, CHANNELS)
    same = iota(square, 0) == iota(square, 1)
    gains = jnp.where(same, gain[...].reshape(1, CHANNELS), 0.0)
    scale = jnp.sum(gains, axis=1, keepdims=True)
    hidden = silu(values * lax.rsqrt(mean + 1e-6) * scale).astype(BF16)
    field[...] = hidden
    pair_sums(1, 0, ids, hidden, pieces, pair, group, products)


def rest_kernel(conv, axis, ids, field, *rest):
    *pieces, keep, partner, groups, products = rest
    place_weights(conv, 1, ids, *pieces, groups.at[0])
    place_weights(conv, 2 * ids[2], ids, *pieces, groups.at[1])
    products[...] = multiply(axis, groups[...].reshape(16 * GROUP, CHANNELS), field[...])

    def emit_keep(at, value):
        keep[at, :] = value

    def emit_partner(at, value):
        partner[at, :] = value.astype(BF16)

    taps(products, lambda slot: (8 + slot) * GROUP, emit_partner)
    taps(products, lambda slot: slot * GROUP, emit_keep)


def rows_kernel(ids, keep, partners, pair, bias, own, later):
    c = ids[2]
    position = 2 * ids[1] + c
    total = keep[...] + partners[1 - c].astype(F32)
    row = iota((64, CHANNELS), 0)
    wanted = BLOCK * ids[0] + 6 * (row // 8) + lax.rem(row, 8)
    chosen = (iota((64, CHANNELS), 1) == wanted) & (lax.rem(row, 8) < 6)
    biases = jnp.where(chosen, bias[...].reshape(1, CHANNELS), 0.0)
    column = jnp.sum(biases, axis=1, keepdims=True)
    place = lax.rem(iota((64, 2 * LANES), 1) // 32, 8)

    def finish(got):
        result = total + got
        own[...] = result[:, :LANES] + column
        later[...] = result[:, LANES:].astype(BF16)

    @pl.when((position > 0) & (position < 7))
    def _():
        finish(pair[...].astype(F32))

    @pl.when(position == 0)
    def _():
        finish(jnp.where(place == 0, 0.0, pltpu.roll(pair[...].astype(F32), 32, 1)))

    @pl.when(position == 7)
    def _():
        got = pltpu.roll(pair[...].astype(F32), 2 * LANES - 32, 1)
        finish(jnp.where(place == 7, 0.0, got))


def block_values(own, earlier):
    total = (own[...] + earlier[...].astype(F32)).astype(BF16)
    to, frm = iota((BLOCK, 64), 0), iota((BLOCK, 64), 1)
    pick = (frm == 8 * (to // 6) + lax.rem(to, 6)).astype(BF16)
    return jnp.dot(pick, total, preferred_element_type=F32).astype(BF16)


def middle_kernel(after, own, earlier, middle):
    result = block_values(own, earlier)
    for z in range(8):
        middle[z] = result


def spread_kernel(own, earlier, latent, pieces, kept):
    result = block_values(own, earlier)
    result = result.astype(F32)
    for z in range(8):
        parts = []
        for first in (0, 24):
            for f in range(2):
                at = 256 * f + 32 * z
                parts.append(result[first : first + 24, at : at + 32])
        pieces[z] = jnp.concatenate(parts, axis=1).astype(BF16)
    kept[...] = latent[...]


def finish_kernel(latent, gathered, out):
    halves = gathered[...].reshape(8 * 24, 128)
    frm, to = iota((8 * 24, CHANNELS), 0), iota((8 * 24, CHANNELS), 1)
    conv = jnp.zeros((64, CHANNELS), F32)
    for half in range(2):
        pick = (to == BLOCK * (frm // 24) + lax.rem(frm, 24) + 24 * half).astype(F32).astype(BF16)
        conv += lax.dot_general(
            halves[:, 64 * half : 64 * half + 64],
            pick,
            (((0,), (0,)), ((), ())),
            preferred_element_type=F32,
        )
    out[...] = (latent[...].astype(F32) + conv).astype(BF16)


def swap_cores(value):
    return lax.ppermute(value, "core", [(0, 1), (1, 0)])


def swap_chips(pair):
    swaps = []
    for x in range(4):
        last, first = 2 * x + 1, 2 * ((x + 1) % 4)
        swaps += [(last, first), (first, last)]
    return lax.ppermute(pair, ("x", "core"), swaps)


def exchange(ids, bias, pair, keep, partner):
    partners = lax.all_gather(partner, "core", axis=0)
    own, later = call(
        rows_kernel,
        [shape((64, LANES), F32), shape((64, LANES), BF16)],
        smem=1,
        n=5,
    )(ids, keep, partners, pair, bias)
    return own, lax.ppermute(later, "t", [(i, i + 1) for i in range(7)])


def gather_weights(pieces):
    hops = []
    for x in range(4):
        hops += [(2 * x, 2 * (x ^ 1)), (2 * x + 1, 2 * (x ^ 3) + 1)]
    far = lax.ppermute(pieces, "x", [(x, x ^ 2) for x in range(4)])
    other = swap_cores(far)
    chip = lax.all_gather(pieces, "core", axis=1)
    result = []
    for both in (chip[0], chip[1]):
        near = lax.all_gather(lax.ppermute(both, ("x", "core"), hops), "core", axis=0)
        result.append((both, near, far, other))
    return result


def per_device(latent, gain_one, weight_one, bias_one, gain_two, weight_two, bias_two):
    ids = jnp.stack([lax.axis_index(a) for a in ("z", "x", "core")]).astype(jnp.int32)
    latent = latent.reshape(64, CHANNELS)
    weight_one, weight_two = [
        jnp.transpose(w, (0, 1, 2, 4, 3)).reshape(27, 6, CHANNELS)
        for w in (weight_one, weight_two)
    ]
    half = shape((64, 2 * LANES), BF16)
    sums = [shape((64, 2 * LANES), F32), half]
    group = pltpu.VMEM((8, GROUP, CHANNELS), BF16)
    groups = pltpu.VMEM((2, 8, GROUP, CHANNELS), BF16)
    products = pltpu.VMEM((8 * GROUP, LANES), F32)
    products_rest = pltpu.VMEM((16 * GROUP, LANES), F32)
    rest = lambda conv, axis: call(
        functools.partial(rest_kernel, conv, axis), sums, [groups, products_rest], smem=1, n=6
    )

    hidden, pieces = call(
        first_kernel,
        [
            shape((8, 64, CHANNELS), BF16),
            shape((2, SLOT, CHANNELS), BF16),
        ],
        [
            pltpu.VMEM((64, CHANNELS), BF16),
            pltpu.VMEM((CHANNELS,), F32),
            pltpu.VMEM((2, 27, 6, CHANNELS), BF16),
            pltpu.VMEM((SLOT, CHANNELS), F32),
            pltpu.SemaphoreType.DMA((4,)),
        ],
        hbm=4,
        n=4,
        vmem_limit=60 * 1024 * 1024,
    )(latent, weight_one, weight_two, gain_one)
    weights_one, weights_two = gather_weights(pieces)
    gathered = lax.all_to_all(hidden, "z", 0, 0)
    field, bias_one = call(
        field_kernel,
        [shape((LANES, CHANNELS), BF16), shape((CHANNELS,), F32)],
        n=2,
        flops=10**11,
    )(gathered, bias_one)
    pair = call(pair_one_kernel, half, [group, products], smem=1, n=6)(ids, field, *weights_one)
    own, earlier = exchange(ids, bias_one, swap_chips(pair), *rest(0, 1)(ids, field, *weights_one))
    middle = call(middle_kernel, shape((8, BLOCK, LANES), BF16), anywhere=1, n=3)(
        weights_two[1], own, earlier
    )
    gathered = lax.all_to_all(middle, "z", 0, 0)
    pair, field, bias_two = call(
        pair_two_kernel,
        [half, shape((CHANNELS, LANES), BF16), shape((CHANNELS,), F32)],
        [group, products],
        smem=1,
        n=8,
    )(ids, gathered, gain_two, bias_two, *weights_two)
    own, earlier = exchange(ids, bias_two, swap_chips(pair), *rest(1, 0)(ids, field, *weights_two))
    pieces, kept = call(
        spread_kernel,
        [shape((8, 24, 128), BF16), shape((64, CHANNELS), BF16)],
        n=3,
    )(own, earlier, latent)
    pieces = lax.all_to_all(pieces, "z", 0, 0)
    out = call(finish_kernel, shape((64, CHANNELS), BF16), n=2)(kept, pieces)
    return out.reshape(2, 1, 32, CHANNELS)


def solution(mesh):
    mesh = Mesh(mesh.devices.reshape(8, 8, 4, 2), ("t", "z", "x", "core"))
    rows = ("z", "x", "core")
    kernel = P(None, None, None, None, rows)
    field = P("t", rows, None, None)
    return jax.shard_map(
        per_device,
        mesh=mesh,
        in_specs=(field, P(), kernel, P(), P(), kernel, P()),
        out_specs=field,
        check_vma=False,
    )
```

```python
import functools

import jax
import jax.numpy as jnp
from jax import lax
from jax.experimental import pallas as pl
from jax.experimental.pallas import tpu as pltpu
from jax.sharding import Mesh
from jax.sharding import PartitionSpec as P

CHANNELS = 384
BLOCK = 48
GROUP = 80
SLOT = 3 * GROUP
LANES = 512
VMEM = 48 * 1024 * 1024
F32 = jnp.float32
BF16 = jnp.bfloat16


def call(kernel, out_shape, scratch=(), smem=0, anywhere=0, n=0, vmem_limit=VMEM, flops=0):
    specs = [pl.BlockSpec(memory_space=pltpu.SMEM)] * smem
    specs += [pl.BlockSpec(memory_space=pl.ANY)] * anywhere
    specs += [pl.BlockSpec(memory_space=pltpu.VMEM)] * (n - len(specs))
    multiple = isinstance(out_shape, (list, tuple))
    vmem = pl.BlockSpec(memory_space=pltpu.VMEM)
    return pl.pallas_call(
        kernel,
        out_shape=out_shape,
        in_specs=specs,
        out_specs=[vmem] * len(out_shape) if multiple else vmem,
        scratch_shapes=list(scratch),
        compiler_params=pltpu.CompilerParams(vmem_limit_bytes=vmem_limit),
        cost_estimate=pl.CostEstimate(flops=flops, bytes_accessed=0, transcendentals=0),
    )


def shape(dims, dtype):
    return jax.ShapeDtypeStruct(dims, dtype)


def iota(dims, axis):
    return lax.broadcasted_iota(jnp.int32, dims, axis)


def silu(v):
    return v / (1.0 + jnp.exp(-v))


def first_kernel(latent, weight_one, weight_two, gain, hidden, pieces, rows):
    rows[...] = jnp.zeros_like(rows)
    for conv, weight in enumerate((weight_one, weight_two)):
        for tap in range(27):
            at = GROUP * (tap // 3 % 3) + 8 * (3 * (tap // 9) + tap % 3)
            rows[at : at + 6, :] = weight[tap].astype(F32)
        pieces[conv] = rows[...].astype(BF16)
    values = latent[...].astype(F32)
    mean = jnp.mean(values * values, axis=1, keepdims=True)
    scale = lax.rsqrt(mean + 1e-6) * gain[...].reshape(1, CHANNELS)
    result = silu(values * scale).astype(BF16)
    for z in range(8):
        hidden[z] = result


def place_weights(conv, height, ids, both, near, far, other, group):
    x, c = ids[1], ids[2]
    across = jnp.bitwise_xor(x, 2)
    rows = pl.ds(pl.multiple_of(GROUP * height, 16), GROUP)
    for i in range(2):
        group[2 * x + i] = both[i, rows, :]
        group[2 * jnp.bitwise_xor(x, 1) + i] = near[0, i, rows, :]
        group[2 * jnp.bitwise_xor(x, 3) + i] = near[1, i, rows, :]
    group[2 * across + c] = far[conv, rows, :]
    group[2 * across + 1 - c] = other[conv, rows, :]


def taps(products, first, emit):
    column = lax.rem(iota((8, 2 * LANES), 1), 32)
    half = LANES // 2
    for two in range(4):
        rows = []
        for slot in (2 * two, 2 * two + 1):
            sums = []
            for l in range(3):
                k = [products[pl.ds(first(slot) + 8 * (3 * i + l), 8), :] for i in range(3)]
                frames = [
                    k[2][:, :half],
                    k[2][:, half:] + k[1][:, :half],
                    k[1][:, half:] + k[0][:, :half],
                    k[0][:, half:],
                ]
                sums.append(jnp.concatenate(frames, axis=1))
            left = jnp.where(column == 0, 0.0, pltpu.roll(sums[0], 1, 1))
            right = jnp.where(column == 31, 0.0, pltpu.roll(sums[2], 2 * LANES - 1, 1))
            rows.append(sums[1] + left + right)
        emit(pl.ds(16 * two, 16), jnp.concatenate(rows, axis=0))


def multiply(axis, group, field):
    return lax.dot_general(
        group, field, (((1,), (axis,)), ((), ())), preferred_element_type=F32
    )


def pair_sums(conv, axis, ids, field, pieces, pair, group, products):
    place_weights(conv, 2 - 2 * ids[2], ids, *pieces, group)
    products[...] = multiply(axis, group[...].reshape(8 * GROUP, CHANNELS), field)

    def emit(at, value):
        pair[at, :] = value.astype(BF16)

    taps(products, lambda slot: slot * GROUP, emit)


def field_kernel(gathered, bias, field, kept):
    kept[...] = bias[...]
    for z in range(8):
        for f in range(2):
            field[pl.ds(256 * f + 32 * z, 32), :] = gathered[z, pl.ds(32 * f, 32), :]


def pair_one_kernel(ids, field, *rest):
    *pieces, pair, group, products = rest
    pair_sums(0, 1, ids, field[...], pieces, pair, group, products)


def pair_two_kernel(ids, gathered, gain, bias, *rest):
    *pieces, pair, field, kept, group, products = rest
    kept[...] = bias[...]
    values = gathered[...].reshape(CHANNELS, LANES).astype(F32)
    mean = jnp.mean(values * values, axis=0, keepdims=True)
    square = (CHANNELS, CHANNELS)
    same = iota(square, 0) == iota(square, 1)
    gains = jnp.where(same, gain[...].reshape(1, CHANNELS), 0.0)
    scale = jnp.sum(gains, axis=1, keepdims=True)
    hidden = silu(values * lax.rsqrt(mean + 1e-6) * scale).astype(BF16)
    field[...] = hidden
    pair_sums(1, 0, ids, hidden, pieces, pair, group, products)


def rest_kernel(conv, axis, ids, field, *rest):
    *pieces, keep, partner, groups, products = rest
    place_weights(conv, 1, ids, *pieces, groups.at[0])
    place_weights(conv, 2 * ids[2], ids, *pieces, groups.at[1])
    products[...] = multiply(axis, groups[...].reshape(16 * GROUP, CHANNELS), field[...])

    def emit_keep(at, value):
        keep[at, :] = value

    def emit_partner(at, value):
        partner[at, :] = value.astype(BF16)

    taps(products, lambda slot: (8 + slot) * GROUP, emit_partner)
    taps(products, lambda slot: slot * GROUP, emit_keep)


def rows_kernel(ids, keep, partners, pair, bias, own, later):
    c = ids[2]
    position = 2 * ids[1] + c
    total = keep[...] + partners[1 - c].astype(F32)
    row = iota((64, CHANNELS), 0)
    wanted = BLOCK * ids[0] + 6 * (row // 8) + lax.rem(row, 8)
    chosen = (iota((64, CHANNELS), 1) == wanted) & (lax.rem(row, 8) < 6)
    biases = jnp.where(chosen, bias[...].reshape(1, CHANNELS), 0.0)
    column = jnp.sum(biases, axis=1, keepdims=True)
    place = lax.rem(iota((64, 2 * LANES), 1) // 32, 8)

    def finish(got):
        result = total + got
        own[...] = result[:, :LANES] + column
        later[...] = result[:, LANES:].astype(BF16)

    @pl.when((position > 0) & (position < 7))
    def _():
        finish(pair[...].astype(F32))

    @pl.when(position == 0)
    def _():
        finish(jnp.where(place == 0, 0.0, pltpu.roll(pair[...].astype(F32), 32, 1)))

    @pl.when(position == 7)
    def _():
        got = pltpu.roll(pair[...].astype(F32), 2 * LANES - 32, 1)
        finish(jnp.where(place == 7, 0.0, got))


def block_values(own, earlier):
    total = (own[...] + earlier[...].astype(F32)).astype(BF16)
    to, frm = iota((BLOCK, 64), 0), iota((BLOCK, 64), 1)
    pick = (frm == 8 * (to // 6) + lax.rem(to, 6)).astype(BF16)
    return jnp.dot(pick, total, preferred_element_type=F32).astype(BF16)


def middle_kernel(after, own, earlier, middle):
    result = block_values(own, earlier)
    for z in range(8):
        middle[z] = result


def spread_kernel(own, earlier, latent, pieces, kept):
    result = block_values(own, earlier)
    for z in range(8):
        frames = [result[:, 256 * f + 32 * z : 256 * f + 32 * z + 32] for f in range(2)]
        pieces[z] = jnp.concatenate(frames, axis=1)
    kept[...] = latent[...]


def finish_kernel(latent, gathered, out):
    square = (CHANNELS, CHANNELS)
    same = iota(square, 0) == iota(square, 1)
    conv = lax.dot_general(
        gathered[...].reshape(CHANNELS, 64),
        same.astype(BF16),
        (((0,), (0,)), ((), ())),
        preferred_element_type=F32,
    )
    out[...] = (latent[...].astype(F32) + conv).astype(BF16)


def swap_cores(value):
    return lax.ppermute(value, "core", [(0, 1), (1, 0)])


def swap_chips(pair):
    swaps = []
    for x in range(4):
        last, first = 2 * x + 1, 2 * ((x + 1) % 4)
        swaps += [(last, first), (first, last)]
    return lax.ppermute(pair, ("x", "core"), swaps)


def exchange(ids, bias, pair, keep, partner):
    partners = lax.all_gather(partner, "core", axis=0)
    own, later = call(
        rows_kernel,
        [shape((64, LANES), F32), shape((64, LANES), BF16)],
        smem=1,
        n=5,
    )(ids, keep, partners, pair, bias)
    return own, lax.ppermute(later, "t", [(i, i + 1) for i in range(7)])


def gather_weights(pieces):
    hops = []
    for x in range(4):
        hops += [(2 * x, 2 * (x ^ 1)), (2 * x + 1, 2 * (x ^ 3) + 1)]
    far = lax.ppermute(pieces, "x", [(x, x ^ 2) for x in range(4)])
    other = swap_cores(far)
    chip = lax.all_gather(pieces, "core", axis=1)
    result = []
    for both in (chip[0], chip[1]):
        near = lax.all_gather(lax.ppermute(both, ("x", "core"), hops), "core", axis=0)
        result.append((both, near, far, other))
    return result


def per_device(latent, gain_one, weight_one, bias_one, gain_two, weight_two, bias_two):
    ids = jnp.stack([lax.axis_index(a) for a in ("z", "x", "core")]).astype(jnp.int32)
    latent = latent.reshape(64, CHANNELS)
    weight_one, weight_two = [
        jnp.transpose(w, (0, 1, 2, 4, 3)).reshape(27, 6, CHANNELS)
        for w in (weight_one, weight_two)
    ]
    half = shape((64, 2 * LANES), BF16)
    sums = [shape((64, 2 * LANES), F32), half]
    group = pltpu.VMEM((8, GROUP, CHANNELS), BF16)
    groups = pltpu.VMEM((2, 8, GROUP, CHANNELS), BF16)
    products = pltpu.VMEM((8 * GROUP, LANES), F32)
    products_rest = pltpu.VMEM((16 * GROUP, LANES), F32)
    rest = lambda conv, axis: call(
        functools.partial(rest_kernel, conv, axis), sums, [groups, products_rest], smem=1, n=6
    )

    hidden, pieces = call(
        first_kernel,
        [shape((8, 64, CHANNELS), BF16), shape((2, SLOT, CHANNELS), BF16)],
        [pltpu.VMEM((SLOT, CHANNELS), F32)],
        n=4,
        vmem_limit=60 * 1024 * 1024,
    )(latent, weight_one, weight_two, gain_one)
    weights_one, weights_two = gather_weights(pieces)
    gathered = lax.all_to_all(hidden, "z", 0, 0)
    field, bias_one = call(
        field_kernel,
        [shape((LANES, CHANNELS), BF16), shape((CHANNELS,), F32)],
        n=2,
        flops=10**11,
    )(gathered, bias_one)
    pair = call(pair_one_kernel, half, [group, products], smem=1, n=6)(ids, field, *weights_one)
    own, earlier = exchange(ids, bias_one, swap_chips(pair), *rest(0, 1)(ids, field, *weights_one))
    middle = call(middle_kernel, shape((8, BLOCK, LANES), BF16), anywhere=1, n=3)(
        weights_two[1], own, earlier
    )
    gathered = lax.all_to_all(middle, "z", 0, 0)
    pair, field, bias_two = call(
        pair_two_kernel,
        [half, shape((CHANNELS, LANES), BF16), shape((CHANNELS,), F32)],
        [group, products],
        smem=1,
        n=8,
    )(ids, gathered, gain_two, bias_two, *weights_two)
    own, earlier = exchange(ids, bias_two, swap_chips(pair), *rest(1, 0)(ids, field, *weights_two))
    pieces, kept = call(
        spread_kernel,
        [shape((8, BLOCK, 64), BF16), shape((64, CHANNELS), BF16)],
        n=3,
    )(own, earlier, latent)
    pieces = lax.all_to_all(pieces, "z", 0, 0)
    out = call(finish_kernel, shape((64, CHANNELS), BF16), n=2)(kept, pieces)
    return out.reshape(2, 1, 32, CHANNELS)


def solution(mesh):
    mesh = Mesh(mesh.devices.reshape(8, 8, 4, 2), ("t", "z", "x", "core"))
    rows = ("z", "x", "core")
    kernel = P(None, None, None, None, rows)
    field = P("t", rows, None, None)
    return jax.shard_map(
        per_device,
        mesh=mesh,
        in_specs=(field, P(), kernel, P(), P(), kernel, P()),
        out_specs=field,
        check_vma=False,
    )
```

```python
import functools

import jax
import jax.numpy as jnp
from jax import lax
from jax.experimental import pallas as pl
from jax.experimental.pallas import tpu as pltpu
from jax.sharding import Mesh
from jax.sharding import PartitionSpec as P

CHANNELS = 384
BLOCK = 48
GROUP = 80
SLOT = 3 * GROUP
LANES = 512
VMEM = 48 * 1024 * 1024
F32 = jnp.float32
BF16 = jnp.bfloat16


def call(kernel, out_shape, scratch=(), smem=0, anywhere=0, n=0, vmem_limit=VMEM, flops=0):
    specs = [pl.BlockSpec(memory_space=pltpu.SMEM)] * smem
    specs += [pl.BlockSpec(memory_space=pl.ANY)] * anywhere
    specs += [pl.BlockSpec(memory_space=pltpu.VMEM)] * (n - len(specs))
    multiple = isinstance(out_shape, (list, tuple))
    vmem = pl.BlockSpec(memory_space=pltpu.VMEM)
    return pl.pallas_call(
        kernel,
        out_shape=out_shape,
        in_specs=specs,
        out_specs=[vmem] * len(out_shape) if multiple else vmem,
        scratch_shapes=list(scratch),
        compiler_params=pltpu.CompilerParams(vmem_limit_bytes=vmem_limit),
        cost_estimate=pl.CostEstimate(flops=flops, bytes_accessed=0, transcendentals=0),
    )


def shape(dims, dtype):
    return jax.ShapeDtypeStruct(dims, dtype)


def iota(dims, axis):
    return lax.broadcasted_iota(jnp.int32, dims, axis)


def silu(v):
    return v / (1.0 + jnp.exp(-v))


def first_kernel(latent, weight_one, weight_two, gain, hidden, pieces, rows):
    rows[...] = jnp.zeros_like(rows)
    for conv, weight in enumerate((weight_one, weight_two)):
        for tap in range(27):
            at = GROUP * (tap // 3 % 3) + 8 * (3 * (tap // 9) + tap % 3)
            rows[at : at + 6, :] = weight[tap].astype(F32)
        pieces[conv] = rows[...].astype(BF16)
    values = latent[...].astype(F32)
    mean = jnp.mean(values * values, axis=1, keepdims=True)
    scale = lax.rsqrt(mean + 1e-6) * gain[...].reshape(1, CHANNELS)
    result = silu(values * scale).astype(BF16)
    for z in range(8):
        hidden[z] = result


def place_weights(conv, height, ids, both, near, far, other, group):
    x, c = ids[1], ids[2]
    across = jnp.bitwise_xor(x, 2)
    rows = pl.ds(pl.multiple_of(GROUP * height, 16), GROUP)
    for i in range(2):
        group[2 * x + i] = both[i, rows, :]
        group[2 * jnp.bitwise_xor(x, 1) + i] = near[0, i, rows, :]
        group[2 * jnp.bitwise_xor(x, 3) + i] = near[1, i, rows, :]
    group[2 * across + c] = far[conv, rows, :]
    group[2 * across + 1 - c] = other[conv, rows, :]


def taps(products, first, emit):
    column = lax.rem(iota((8, 2 * LANES), 1), 32)
    half = LANES // 2
    for two in range(4):
        rows = []
        for slot in (2 * two, 2 * two + 1):
            sums = []
            for l in range(3):
                k = [products[pl.ds(first(slot) + 8 * (3 * i + l), 8), :] for i in range(3)]
                frames = [
                    k[2][:, :half],
                    k[2][:, half:] + k[1][:, :half],
                    k[1][:, half:] + k[0][:, :half],
                    k[0][:, half:],
                ]
                sums.append(jnp.concatenate(frames, axis=1))
            left = jnp.where(column == 0, 0.0, pltpu.roll(sums[0], 1, 1))
            right = jnp.where(column == 31, 0.0, pltpu.roll(sums[2], 2 * LANES - 1, 1))
            rows.append(sums[1] + left + right)
        emit(pl.ds(16 * two, 16), jnp.concatenate(rows, axis=0))


def multiply(axis, group, field):
    return lax.dot_general(
        group, field, (((1,), (axis,)), ((), ())), preferred_element_type=F32
    )


def pair_sums(conv, axis, ids, field, pieces, pair, group, products):
    place_weights(conv, 2 - 2 * ids[2], ids, *pieces, group)
    products[...] = multiply(axis, group[...].reshape(8 * GROUP, CHANNELS), field)

    def emit(at, value):
        pair[at, :] = value.astype(BF16)

    taps(products, lambda slot: slot * GROUP, emit)


def field_kernel(gathered, bias, field, kept):
    kept[...] = bias[...]
    for z in range(8):
        for f in range(2):
            field[pl.ds(256 * f + 32 * z, 32), :] = gathered[z, pl.ds(32 * f, 32), :]


def pair_one_kernel(ids, field, *rest):
    *pieces, pair, group, products = rest
    pair_sums(0, 1, ids, field[...], pieces, pair, group, products)


def pair_two_kernel(ids, gathered, gain, bias, *rest):
    *pieces, pair, field, kept, group, products = rest
    kept[...] = bias[...]
    values = gathered[...].reshape(CHANNELS, LANES).astype(F32)
    mean = jnp.mean(values * values, axis=0, keepdims=True)
    square = (CHANNELS, CHANNELS)
    same = iota(square, 0) == iota(square, 1)
    gains = jnp.where(same, gain[...].reshape(1, CHANNELS), 0.0)
    scale = jnp.sum(gains, axis=1, keepdims=True)
    hidden = silu(values * lax.rsqrt(mean + 1e-6) * scale).astype(BF16)
    field[...] = hidden
    pair_sums(1, 0, ids, hidden, pieces, pair, group, products)


def rest_kernel(conv, axis, ids, field, *rest):
    *pieces, keep, partner, groups, products = rest
    place_weights(conv, 1, ids, *pieces, groups.at[0])
    place_weights(conv, 2 * ids[2], ids, *pieces, groups.at[1])
    products[...] = multiply(axis, groups[...].reshape(16 * GROUP, CHANNELS), field[...])

    def emit_keep(at, value):
        keep[at, :] = value

    def emit_partner(at, value):
        partner[at, :] = value.astype(BF16)

    taps(products, lambda slot: (8 + slot) * GROUP, emit_partner)
    taps(products, lambda slot: slot * GROUP, emit_keep)


def rows_kernel(ids, keep, partners, pair, bias, own, later):
    c = ids[2]
    position = 2 * ids[1] + c
    total = keep[...] + partners[1 - c].astype(F32)
    row = iota((64, CHANNELS), 0)
    wanted = BLOCK * ids[0] + 6 * (row // 8) + lax.rem(row, 8)
    chosen = (iota((64, CHANNELS), 1) == wanted) & (lax.rem(row, 8) < 6)
    biases = jnp.where(chosen, bias[...].reshape(1, CHANNELS), 0.0)
    column = jnp.sum(biases, axis=1, keepdims=True)
    place = lax.rem(iota((64, 2 * LANES), 1) // 32, 8)

    def finish(got):
        result = total + got
        own[...] = result[:, :LANES] + column
        later[...] = result[:, LANES:].astype(BF16)

    @pl.when((position > 0) & (position < 7))
    def _():
        finish(pair[...].astype(F32))

    @pl.when(position == 0)
    def _():
        finish(jnp.where(place == 0, 0.0, pltpu.roll(pair[...].astype(F32), 32, 1)))

    @pl.when(position == 7)
    def _():
        got = pltpu.roll(pair[...].astype(F32), 2 * LANES - 32, 1)
        finish(jnp.where(place == 7, 0.0, got))


def block_values(own, earlier):
    total = (own[...] + earlier[...].astype(F32)).astype(BF16)
    to, frm = iota((BLOCK, 64), 0), iota((BLOCK, 64), 1)
    pick = (frm == 8 * (to // 6) + lax.rem(to, 6)).astype(BF16)
    return jnp.dot(pick, total, preferred_element_type=F32).astype(BF16)


def middle_kernel(after, own, earlier, middle):
    result = block_values(own, earlier)
    for z in range(8):
        middle[z] = result


def spread_kernel(own, earlier, latent, pieces, kept):
    result = block_values(own, earlier)
    for z in range(8):
        frames = [result[:, 256 * f + 32 * z : 256 * f + 32 * z + 32] for f in range(2)]
        pieces[z] = jnp.concatenate(frames, axis=1)
    kept[...] = latent[...]


def finish_kernel(latent, gathered, out):
    square = (CHANNELS, CHANNELS)
    same = iota(square, 0) == iota(square, 1)
    conv = lax.dot_general(
        gathered[...].reshape(CHANNELS, 64),
        same.astype(BF16),
        (((0,), (0,)), ((), ())),
        preferred_element_type=F32,
    )
    out[...] = (latent[...].astype(F32) + conv).astype(BF16)


def swap_cores(value):
    return lax.ppermute(value, "core", [(0, 1), (1, 0)])


def swap_chips(pair):
    swaps = []
    for x in range(4):
        last, first = 2 * x + 1, 2 * ((x + 1) % 4)
        swaps += [(last, first), (first, last)]
    return lax.ppermute(pair, ("x", "core"), swaps)


def exchange(ids, bias, pair, keep, partner):
    partners = lax.all_gather(partner, "core", axis=0)
    own, later = call(
        rows_kernel,
        [shape((64, LANES), F32), shape((64, LANES), BF16)],
        smem=1,
        n=5,
    )(ids, keep, partners, pair, bias)
    return own, lax.ppermute(later, "t", [(i, i + 1) for i in range(7)])


def gather_weights(pieces):
    hops = []
    for x in range(4):
        hops += [(2 * x, 2 * (x ^ 1)), (2 * x + 1, 2 * (x ^ 3) + 1)]
    far = lax.ppermute(pieces, "x", [(x, x ^ 2) for x in range(4)])
    other = swap_cores(far)
    chip = lax.all_gather(pieces, "core", axis=1)
    result = []
    for both in (chip[0], chip[1]):
        near = lax.all_gather(lax.ppermute(both, ("x", "core"), hops), "core", axis=0)
        result.append((both, near, far, other))
    return result


def per_device(latent, gain_one, weight_one, bias_one, gain_two, weight_two, bias_two):
    ids = jnp.stack([lax.axis_index(a) for a in ("z", "x", "core")]).astype(jnp.int32)
    latent = latent.reshape(64, CHANNELS)
    weight_one, weight_two = [
        jnp.transpose(w, (0, 1, 2, 4, 3)).reshape(27, 6, CHANNELS)
        for w in (weight_one, weight_two)
    ]
    half = shape((64, 2 * LANES), BF16)
    sums = [shape((64, 2 * LANES), F32), half]
    group = pltpu.VMEM((8, GROUP, CHANNELS), BF16)
    groups = pltpu.VMEM((2, 8, GROUP, CHANNELS), BF16)
    products = pltpu.VMEM((8 * GROUP, LANES), F32)
    products_rest = pltpu.VMEM((16 * GROUP, LANES), F32)
    rest = lambda conv, axis: call(
        functools.partial(rest_kernel, conv, axis), sums, [groups, products_rest], smem=1, n=6
    )

    hidden, pieces = call(
        first_kernel,
        [shape((8, 64, CHANNELS), BF16), shape((2, SLOT, CHANNELS), BF16)],
        [pltpu.VMEM((SLOT, CHANNELS), F32)],
        n=4,
        vmem_limit=60 * 1024 * 1024,
    )(latent, weight_one, weight_two, gain_one)
    weights_one, weights_two = gather_weights(pieces)
    gathered = lax.all_to_all(hidden, "z", 0, 0)
    field, bias_one = call(
        field_kernel,
        [shape((LANES, CHANNELS), BF16), shape((CHANNELS,), F32)],
        n=2,
        flops=10**11,
    )(gathered, bias_one)
    pair = call(pair_one_kernel, half, [group, products], smem=1, n=6)(ids, field, *weights_one)
    own, earlier = exchange(ids, bias_one, swap_chips(pair), *rest(0, 1)(ids, field, *weights_one))
    middle = call(middle_kernel, shape((8, BLOCK, LANES), BF16), anywhere=1, n=3)(
        weights_two[2], own, earlier
    )
    gathered = lax.all_to_all(middle, "z", 0, 0)
    pair, field, bias_two = call(
        pair_two_kernel,
        [half, shape((CHANNELS, LANES), BF16), shape((CHANNELS,), F32)],
        [group, products],
        smem=1,
        n=8,
    )(ids, gathered, gain_two, bias_two, *weights_two)
    own, earlier = exchange(ids, bias_two, swap_chips(pair), *rest(1, 0)(ids, field, *weights_two))
    pieces, kept = call(
        spread_kernel,
        [shape((8, BLOCK, 64), BF16), shape((64, CHANNELS), BF16)],
        n=3,
    )(own, earlier, latent)
    pieces = lax.all_to_all(pieces, "z", 0, 0)
    out = call(finish_kernel, shape((64, CHANNELS), BF16), n=2)(kept, pieces)
    return out.reshape(2, 1, 32, CHANNELS)


def solution(mesh):
    mesh = Mesh(mesh.devices.reshape(8, 8, 4, 2), ("t", "z", "x", "core"))
    rows = ("z", "x", "core")
    kernel = P(None, None, None, None, rows)
    field = P("t", rows, None, None)
    return jax.shard_map(
        per_device,
        mesh=mesh,
        in_specs=(field, P(), kernel, P(), P(), kernel, P()),
        out_specs=field,
        check_vma=False,
    )
```
